256 devices in a mesh: dp: 64 (over z, x_lo, y), mp: 4 (over x_hi, core).
Axes of the slice: x: 4 (x_hi: 2, x_lo: 2; x = x_hi * 2 + x_lo), y: 4, z: 8, core: 2. Of those that a mesh axis runs over, the one named last changes fastest.
Arguments:
- image_feats: bfloat16 [8704, 1536], P('dp'), may hold values from -16 to 16
- text_feats: bfloat16 [8704, 1152], P('dp'), may hold values from -16 to 16
- image_head: bfloat16 [1536, 1536], P(None, 'mp'), may hold values from -0.15625 to 0.15625
- text_head: bfloat16 [1152, 1536], P(None, 'mp'), may hold values from -0.1875 to 0.1875
- log_temp: float32 [1], replicated, may hold values from 1.5 to 2.5
- logit_bias: float32 [1], replicated, may hold values from -4 to -1
Outputs:
- image_head_grad: float32 [1536, 1536], P('dp', 'mp')
- text_head_grad: float32 [1152, 1536], P('dp', 'mp')
The draws below stay inside these ranges and needn't reach their ends.
All inputs are finite; a program needn't handle non-finite values.
Results may differ from the reference program's by a relative error of at most 0.004.
Values may be sent and summed in bfloat16 or wider, within the bound.
A program may use at most 128 MiB of HBM per device.

```python
import jax
import jax.numpy as jnp
from jax import lax

WI = 1536
WT = 1152
E = 1536
BD = 136
B = 8704
N_DP = 64


def spiked(array, stream_key, source, target, blocks, factor):
    def block_of(axis_at):
        return (jnp.arange(array.shape[axis_at]) // (array.shape[axis_at] // blocks)).reshape((-1,) + (1,) * (array.ndim - 1 - axis_at))

    first = jax.random.permutation(stream_key, blocks)[block_of(target)]
    other_side = (block_of(target) + blocks // 2) % blocks
    return jnp.where((block_of(source) == first) | (block_of(source) == other_side), factor * array, array)


def level_of(stream_key, shape, shards, low, largest):
    gain = 1.0
    for axis_at, shards_of in shards:
        steps = jax.random.uniform(jax.random.fold_in(jax.random.fold_in(stream_key, 6), axis_at), (shards_of,), jnp.float32, low / len(shards), largest / len(shards))
        gain = gain * jnp.repeat(jnp.exp(steps), shape[axis_at] // shards_of).reshape((-1,) + (1,) * (len(shape) - 1 - axis_at))
    return gain


def centred(rng, shape, spread, bound, shards=(), kind=jnp.bfloat16):
    entries = jax.random.normal(rng, shape, jnp.float32) * spread
    if len(shards) > 0:
        entries = level_of(rng, shape, shards, -0.22, 0.18) * entries
    return jnp.clip(entries, min=-bound, max=bound).astype(kind)


def gaussian_with(own_key, shape, spread, bound, split, heavy, kind=jnp.bfloat16):
    array = spread * jax.random.normal(own_key, shape, jnp.float32)
    if split:
        array = array * level_of(own_key, shape, split, -0.22, 0.18)
    return jnp.clip(spiked(array, jax.random.fold_in(own_key, 3), *heavy), -bound, bound).astype(kind)


def setup_inputs(seed: int = 0) -> dict:
    key_of = jax.random.split(jax.random.key(seed), 7)
    image_feats = gaussian_with(key_of[0], (B, WI), 1.0, 16.0, ((0, 64),), (0, 1, 64, 4.0))
    text_feats = gaussian_with(key_of[1], (B, WT), 1.0, 16.0, ((0, 64),), (0, 1, 64, 4.0))
    image_head = centred(key_of[2], (WI, E), WI ** -0.5, 0.15625, ((1, 4),))
    text_head = centred(key_of[3], (WT, E), WT ** -0.5, 0.1875, ((1, 4),))
    log_temp = jnp.clip(jax.random.uniform(key_of[4], (1,), jnp.float32, 1.5, 2.5), 1.5, 2.5)
    logit_bias = jnp.clip(jax.random.uniform(key_of[5], (1,), jnp.float32, -4.0, -1.0), -4.0, -1.0)
    return dict(image_feats=image_feats, text_feats=text_feats, image_head=image_head, text_head=text_head, log_temp=log_temp, logit_bias=logit_bias)


def unit_rows(pre_act):
    row_norm = jnp.sqrt(lax.optimization_barrier(jnp.sum(pre_act * pre_act, axis=1)) + 1e-06)
    return (pre_act / row_norm[:, None], row_norm)

def reference(image_feats, text_feats, image_head, text_head, log_temp, logit_bias):
    img_pre = jnp.dot(image_feats, image_head, preferred_element_type=jnp.float32)
    txt_pre = jnp.dot(text_feats, text_head, preferred_element_type=jnp.float32)
    img_dir, img_norm = unit_rows(img_pre)
    txt_dir, txt_norm = unit_rows(txt_pre)
    img_unit = img_dir.astype(jnp.bfloat16)
    txt_unit = txt_dir.astype(jnp.bfloat16)
    temper = jnp.exp(log_temp[0])
    column_ids = jnp.arange(B, dtype=jnp.int32)[None, :]
    blocks = img_unit.reshape(N_DP, BD, E)
    block_ids = jnp.arange(N_DP, dtype=jnp.int32)

    def block_step(carry, inputs):
        img_block, block_id = inputs
        logits = temper * jnp.dot(img_block, txt_unit.T, preferred_element_type=jnp.float32) + logit_bias[0]
        row_ids = block_id * BD + jnp.arange(BD, dtype=jnp.int32)[:, None]
        pair_grad = (temper * (jax.nn.sigmoid(logits) - (column_ids == row_ids).astype(jnp.float32))).astype(jnp.bfloat16)
        img_block_grad = jnp.dot(pair_grad, txt_unit, preferred_element_type=jnp.float32)
        carry = carry + jnp.dot(pair_grad.T, img_block, preferred_element_type=jnp.float32)
        return (carry, img_block_grad)
    txt_unit_grad, img_parts = lax.scan(block_step, jnp.zeros((B, E), jnp.float32), (blocks, block_ids))
    img_unit_grad = img_parts.reshape(B, E)
    img_along = lax.optimization_barrier(jnp.sum(img_unit_grad * img_dir, axis=1))
    txt_along = lax.optimization_barrier(jnp.sum(txt_unit_grad * txt_dir, axis=1))
    img_grad = ((img_unit_grad - img_dir * img_along[:, None]) / img_norm[:, None]).astype(jnp.bfloat16)
    txt_grad = ((txt_unit_grad - txt_dir * txt_along[:, None]) / txt_norm[:, None]).astype(jnp.bfloat16)
    image_head_grad = jnp.dot(image_feats.T, img_grad, preferred_element_type=jnp.float32)
    text_head_grad = jnp.dot(text_feats.T, txt_grad, preferred_element_type=jnp.float32)
    return (image_head_grad, text_head_grad)
```

```python
import jax
import jax.numpy as jnp
from jax import lax
from jax.experimental import pallas as pl
from jax.experimental.pallas import tpu as pltpu
from jax.sharding import PartitionSpec as P

F32 = jnp.float32
BF16 = jnp.bfloat16
MESH = pl.DeviceIdType.MESH
NT = (((1,), (1,)), ((), ()))
TN = (((0,), (0,)), ((), ()))
NN = (((1,), (0,)), ((), ()))
R = 136
RT = 144
RI = 80
W = 384
MESSAGES = 160


def kernel(
    xf, tf, xh_ref, th_ref, log_temp, logit_bias, out_i, out_t,
    sums, norm_b, dir_t, dir_i, parts, texts, images, mine, theirs, pg, grad_i, grad_t, grad_tb,
    ring_s, ring_r, half_s, half_r, ta_r, tb_r, ta_sum, tb_sum, ta_s, tb_s, ta_r2, tb_r2,
    along, head_t, head_i, ht_s0, ht_r0, ht_s1, ht_r1, xt, xt_r, si, ri, zi, zi_r,
    send_sem, recv_sem,
):
    dp, mp = lax.axis_index("dp"), lax.axis_index("mp")
    z, xl, y = lax.div(dp, 8), lax.rem(lax.div(dp, 4), 2), lax.rem(dp, 4)
    xh, core = lax.div(mp, 2), lax.rem(mp, 2)
    x = xh * 2 + xl

    def at(z_at=None, x_at=None, y_at=None, core_at=None):
        z_at = z if z_at is None else z_at
        x_at = x if x_at is None else x_at
        y_at = y if y_at is None else y_at
        core_at = core if core_at is None else core_at
        return (
            (z_at * 2 + lax.rem(x_at, 2)) * 4 + y_at,
            lax.div(x_at, 2) * 2 + core_at,
        )

    def zo(o):
        return lax.rem(z + o + 8, 8)

    def xo(o):
        return lax.rem(x + o + 4, 4)

    def yo(o):
        return lax.rem(y + o + 4, 4)

    started = []

    def message(src, dst, where):
        k = len(started)
        copy = pltpu.make_async_remote_copy(
            src_ref=src, dst_ref=dst, send_sem=send_sem.at[k], recv_sem=recv_sem.at[k],
            device_id=where, device_id_type=MESH,
        )
        copy.start()
        started.append(copy)
        return copy

    def lanes(half):
        return pl.ds(pl.multiple_of(half * W, 128), W)

    barrier = pltpu.get_barrier_semaphore()
    peers = [at(x_at=xo(a), y_at=yo(b)) for a in range(4) for b in range(4) if a or b]
    peers += [at(z_at=zo(o)) for o in range(1, 8)]
    peers += [at(core_at=1 - core), at(x_at=xo(2), core_at=1 - core)]
    for peer in peers:
        pl.semaphore_signal(barrier, inc=1, device_id=peer, device_id_type=MESH)

    def padded(value, rows):
        return jnp.concatenate([value, jnp.zeros((rows - value.shape[0],) + value.shape[1:], value.dtype)], axis=0)

    txt_pre = jnp.dot(tf[...], th_ref[...], preferred_element_type=F32)
    dir_t[...] = padded(txt_pre, RT)
    img_pre = jnp.dot(xf[...], xh_ref[...], preferred_element_type=F32)
    dir_i[...] = padded(img_pre, RT)
    left = lax.broadcasted_iota(jnp.int32, (RT, 128), 1) < 64

    def two_sums(a, b):
        return jnp.where(left, jnp.sum(a, axis=1, keepdims=True), jnp.sum(b, axis=1, keepdims=True))

    def over_mp(ref, value):
        ref[mp] = value
        got = [
            message(ref.at[mp], ref.at[mp], where)
            for where in (at(core_at=1 - core), at(x_at=xo(2)), at(x_at=xo(2), core_at=1 - core))
        ]
        for copy in got:
            copy.wait_recv()
        return (ref[0] + ref[1]) + (ref[2] + ref[3])

    a, b = dir_t[...], dir_i[...]
    value = two_sums(a * a, b * b)
    pl.semaphore_wait(barrier, len(peers))
    norms = jnp.sqrt(over_mp(sums, value) + 1e-06)
    txt_norm, img_norm = norms[:, 0:1], norms[:, 64:65]
    txt_dir = dir_t[...] / txt_norm
    img_dir = dir_i[...] / img_norm
    dir_t[...] = txt_dir
    dir_i[...] = img_dir
    norm_b[...] = norms

    slot = xl * 4 + y
    own, other = lanes(xh), lanes(1 - xh)
    texts[slot, :, own] = txt_dir.astype(BF16)
    low, high = pl.ds(0, 64), pl.ds(64, 80)
    stage_a = [message(texts.at[slot, low, own], texts.at[slot, low, own], at(x_at=xo(o))) for o in (1, 2, 3)]
    stage_b = [message(texts.at[slot, high, own], texts.at[slot, high, own], at(y_at=yo(o))) for o in (1, 2, 3)]
    parts[0] = padded(img_dir[0:64], RI).astype(BF16)
    parts[1] = img_dir[64:144].astype(BF16)
    swap = message(parts.at[1 - xh], images.at[z, :, own], at(x_at=xo(2)))
    images[z, :, own] = parts[xh]
    up, down = at(z_at=zo(1)), at(z_at=zo(-1))
    kinds = (own, other)
    ups, downs = {}, {}
    for q in (0, 1):
        if q == 1:
            swap.wait_recv()
        ups[q, 1] = message(images.at[z, :, kinds[q]], images.at[z, :, kinds[q]], up)
        downs[q, 1] = message(images.at[z, :, kinds[q]], images.at[z, :, kinds[q]], down)

    def pass_images(step):
        for q in (0, 1):
            if (q, step) in ups:
                ups[q, step].wait_recv()
                if step < 4 - q:
                    view = images.at[zo(-step), :, kinds[q]]
                    ups[q, step + 1] = message(view, view, up)
            if (q, step) in downs:
                downs[q, step].wait_recv()
                if step < 3 + q:
                    view = images.at[zo(step), :, kinds[q]]
                    downs[q, step + 1] = message(view, view, down)

    for copy in stage_a:
        copy.wait_recv()
    stage_a2 = []
    for o in (1, 2, 3):
        for k in (0, 1):
            view = texts.at[k * 4 + y, low, :]
            stage_a2.append(message(view, view, at(y_at=yo(o))))
    for copy in stage_b:
        copy.wait_recv()
    stage_b2 = []
    for o in (1, 2, 3):
        for k in range(4):
            view = texts.at[xl * 4 + k, high, own]
            stage_b2.append(message(view, view, at(x_at=xo(o))))
    for step in (1, 2, 3, 4):
        pass_images(step)
    for copy in stage_a2 + stage_b2:
        copy.wait_recv()

    all_texts = texts[...].reshape(8 * RT, 2 * W)
    theirs_at = pl.ds((1 - core) * 4, 4)
    mine_at = pl.ds(core * 4, 4)
    theirs[...] = lax.dot_general(
        images[theirs_at].reshape(4 * RI, 2 * W), all_texts, NT, preferred_element_type=F32
    ).reshape(4, RI, 8 * RT)
    cross = message(theirs, mine.at[1], at(core_at=1 - core))
    mine[0] = lax.dot_general(
        images[mine_at].reshape(4 * RI, 2 * W), all_texts, NT, preferred_element_type=F32
    ).reshape(4, RI, 8 * RT)
    cross.wait_recv()
    temper = jnp.exp(jnp.full((1, 128), log_temp[0], F32))[:, 0:1]
    bias = logit_bias[0]
    ahead = lax.broadcasted_iota(jnp.int32, (RI, 8 * RT), 1) - lax.broadcasted_iota(jnp.int32, (RI, 8 * RT), 0)

    @pl.loop(0, 4)
    def _(block):
        logits = temper * (mine[0, block] + mine[1, block]) + bias
        same = ahead == jnp.where(core * 4 + block == z, slot * RT + 64 * xh, -8192)
        pg[core * 4 + block] = (temper * (jax.nn.sigmoid(logits) - same.astype(F32))).astype(BF16)

    share = message(pg.at[mine_at], pg.at[mine_at], at(core_at=1 - core))
    share.wait_recv()
    every = pg[...].reshape(8 * RI, 8 * RT)
    grad_i[...] = lax.dot_general(every, all_texts, NN, preferred_element_type=F32).reshape(8, RI, 2 * W)
    grad_t[...] = lax.dot_general(
        every, images[...].reshape(8 * RI, 2 * W), TN, preferred_element_type=F32
    ).reshape(8, RT, 2 * W)

    grad_tb[...] = grad_t[...].astype(BF16)
    back_a, back_b = {}, {}
    for o in (1, 2, 3):
        for k in (0, 1):
            back_a[o, k] = message(grad_tb.at[k * 4 + yo(o), low, :], ta_r.at[o - 1, k], at(y_at=yo(o)))
    for o in (1, 2, 3):
        to = xo(o)
        for k in range(4):
            back_b[o, k] = message(
                grad_tb.at[lax.rem(to, 2) * 4 + k, high, lanes(lax.div(to, 2))], tb_r.at[o - 1, k], at(x_at=to)
            )

    def ring(piece, send, recv, chain, finish):
        went = {}
        for step in (1, 2, 3, 4):
            for q in (0, 1):
                for way, sign, length in ((0, 1, chain[q]), (1, -1, 7 - chain[q])):
                    first = 5 - length
                    if step < first:
                        continue
                    value = piece(q, zo(sign * (5 - step)))
                    if step > first:
                        went[way, q, step - 1].wait_recv()
                        value = value + recv(q, way, step - 1)[...].astype(F32)
                    send(q, way, step)[...] = value.astype(BF16)
                    went[way, q, step] = message(
                        send(q, way, step), recv(q, way, step), at(z_at=zo(sign))
                    )
        for q in (0, 1):
            total = piece(q, z)
            for way in (0, 1):
                went[way, q, 4].wait_recv()
                total = total + recv(q, way, 4)[...].astype(F32)
            finish(q, total)

    def image_done(q, total):
        if q == 0:
            dir_own[...] = total
        else:
            half_s[...] = total.astype(BF16)

    dir_own = mine.at[0, 0, :, pl.ds(0, W)]
    ring(
        lambda q, to: grad_i[to, :, kinds[q]],
        lambda q, way, step: ring_s.at[q, way, step - 1],
        lambda q, way, step: ring_r.at[q, way, step - 1],
        (4, 3),
        image_done,
    )
    swap_back = message(half_s, half_r, at(x_at=xo(2)))

    for copy in back_a.values():
        copy.wait_recv()
    for k in (0, 1):
        ta_sum[k] = grad_t[k * 4 + y, low, :] + sum(ta_r[o, k].astype(F32) for o in range(3))
    ta_s[...] = ta_sum[...].astype(BF16)
    back_a2 = []
    for o in (1, 2, 3):
        to = xo(o)
        back_a2.append(message(ta_s.at[lax.rem(to, 2), :, lanes(lax.div(to, 2))], ta_r2.at[o - 1], at(x_at=to)))
    for copy in back_b.values():
        copy.wait_recv()
    for k in range(4):
        tb_sum[k] = grad_t[xl * 4 + k, high, own] + sum(tb_r[o, k].astype(F32) for o in range(3))
    tb_s[...] = tb_sum[...].astype(BF16)
    back_b2 = [message(tb_s.at[yo(o)], tb_r2.at[o - 1], at(y_at=yo(o))) for o in (1, 2, 3)]
    for copy in back_a2 + back_b2:
        copy.wait_recv()
    txt_unit_grad = jnp.concatenate(
        [
            ta_sum[xl, :, own] + sum(ta_r2[o].astype(F32) for o in range(3)),
            tb_sum[y] + sum(tb_r2[o].astype(F32) for o in range(3)),
        ],
        axis=0,
    )
    swap_back.wait_recv()
    grad_i[xh, :, pl.ds(0, W)] = dir_own[...]
    grad_i[1 - xh, :, pl.ds(0, W)] = half_r[...].astype(F32)
    img_unit_grad = jnp.concatenate([grad_i[0, pl.ds(0, 64), pl.ds(0, W)], grad_i[1, :, pl.ds(0, W)]], axis=0)

    txt_dir, img_dir, norms = dir_t[...], dir_i[...], norm_b[...]
    alongs = over_mp(along, two_sums(txt_unit_grad * txt_dir, img_unit_grad * img_dir))
    txt_grad = ((txt_unit_grad - txt_dir * alongs[:, 0:1]) / norms[:, 0:1]).astype(BF16)
    img_grad = ((img_unit_grad - img_dir * alongs[:, 64:65]) / norms[:, 64:65]).astype(BF16)

    head_i[...] = lax.dot_general(xf[...], img_grad[0:R], TN, preferred_element_type=F32)
    for j in range(8):
        si[j] = jnp.concatenate([head_i[pl.ds(k * 192 + j * 24, 24), :] for k in range(8)], axis=0).astype(BF16)
    out_xy = {}
    for a in (0, 1):
        for b in range(4):
            if a or b:
                to_xl = lax.rem(xl + a, 2)
                out_xy[a, b] = message(
                    si.at[to_xl * 4 + yo(b)], ri.at[a * 4 + b - 1], at(x_at=xh * 2 + to_xl, y_at=yo(b))
                )
    head_t[...] = lax.dot_general(tf[...], txt_grad[0:R], TN, preferred_element_type=F32)
    sends, recvs = (ht_s0, ht_s1), (ht_r0, ht_r1)
    spans = ((0, 64), (64, 80))

    def text_done(q, total):
        head_t[pl.ds(spans[q][0], spans[q][1]), :] = total

    ring(
        lambda q, to: head_t[pl.ds(pl.multiple_of(to * 144 + spans[q][0], 16), spans[q][1]), :],
        lambda q, way, step: sends[q].at[way, step - 1],
        lambda q, way, step: recvs[q].at[way, step - 1],
        (4, 3),
        text_done,
    )
    total = head_t[pl.ds(0, 144), :]
    for j in range(8):
        xt[j] = padded(total[18 * j : 18 * j + 18], 24)
    last_t = []
    for a in (0, 1):
        for b in range(4):
            if a or b:
                to_xl = lax.rem(xl + a, 2)
                last_t.append(
                    message(xt.at[to_xl * 4 + yo(b)], xt_r.at[a * 4 + b - 1], at(x_at=xh * 2 + to_xl, y_at=yo(b)))
                )
    for copy in out_xy.values():
        copy.wait_recv()
    for k in range(8):
        zi[k] = head_i[pl.ds(pl.multiple_of(k * 192 + slot * 24, 8), 24), :]
    for j in range(7):
        zi[...] = zi[...] + ri[j].astype(F32).reshape(8, 24, W)
    last_i = [message(zi.at[zo(o)], zi_r.at[o - 1], at(z_at=zo(o))) for o in range(1, 8)]
    for copy in last_t:
        copy.wait_recv()
    out_t[...] = (xt[slot] + sum(xt_r[j] for j in range(7)))[0:18]
    for copy in last_i:
        copy.wait_recv()
    out_i[...] = zi[z] + sum(zi_r[j] for j in range(7))
    for copy in started:
        copy.wait_send()


def body(image_feats, text_feats, image_head, text_head, log_temp, logit_bias):
    vmem = pl.BlockSpec(memory_space=pltpu.VMEM)
    smem = pl.BlockSpec(memory_space=pltpu.SMEM)

    def f32(*shape):
        return pltpu.VMEM(shape, F32)

    def bf16(*shape):
        return pltpu.VMEM(shape, BF16)

    scratch = [
        f32(4, RT, 128), f32(RT, 128), f32(RT, W), f32(RT, W),
        bf16(2, RI, W), bf16(8, RT, 2 * W), bf16(8, RI, 2 * W),
        f32(2, 4, RI, 8 * RT), f32(4, RI, 8 * RT), bf16(8, RI, 8 * RT),
        f32(8, RI, 2 * W), f32(8, RT, 2 * W), bf16(8, RT, 2 * W),
        bf16(2, 2, 4, RI, W), bf16(2, 2, 4, RI, W), bf16(RI, W), bf16(RI, W),
        bf16(3, 2, 64, 2 * W), bf16(3, 4, 80, W), f32(2, 64, 2 * W), f32(4, 80, W),
        bf16(2, 64, 2 * W), bf16(4, 80, W), bf16(3, 64, W), bf16(3, 80, W),
        f32(4, RT, 128), f32(1152, W), f32(1536, W),
        bf16(2, 4, 64, W), bf16(2, 4, 64, W), bf16(2, 4, 80, W), bf16(2, 4, 80, W),
        f32(8, 24, W), f32(7, 24, W), bf16(8, 192, W), bf16(7, 192, W), f32(8, 24, W), f32(7, 24, W),
        pltpu.SemaphoreType.DMA((MESSAGES,)), pltpu.SemaphoreType.DMA((MESSAGES,)),
    ]
    return pl.pallas_call(
        kernel,
        out_shape=(jax.ShapeDtypeStruct((24, W), F32), jax.ShapeDtypeStruct((18, W), F32)),
        in_specs=[vmem, vmem, vmem, vmem, smem, smem],
        out_specs=(vmem, vmem),
        scratch_shapes=scratch,
        compiler_params=pltpu.CompilerParams(
            collective_id=0, has_side_effects=True, vmem_limit_bytes=56 * 1024 * 1024
        ),
        name="pair_loss",
    )(image_feats, text_feats, image_head, text_head, log_temp, logit_bias)


def solution(mesh):
    placed = (P("dp", None), P("dp", None), P(None, "mp"), P(None, "mp"), P(), P())
    return jax.shard_map(
        body, mesh=mesh, in_specs=placed, out_specs=(P("dp", "mp"), P("dp", "mp")), check_vma=False
    )
```

```python
import types

import jax
import jax.numpy as jnp
from jax import lax
from jax.experimental import pallas as pl
from jax.experimental.pallas import tpu as pltpu
from jax.sharding import PartitionSpec as P

F32 = jnp.float32
BF16 = jnp.bfloat16
MESH = pl.DeviceIdType.MESH
NT = (((1,), (1,)), ((), ()))
TN = (((0,), (0,)), ((), ()))
NN = (((1,), (0,)), ((), ()))
R = 136
RT = 144
RI = 80
W = 384
MESSAGES = 200
RA, RB = 64, 80
I_CHUNKS = ((0, (0, 48)), (0, (48, 32)), (1, (0, 48)), (1, (48, 32)))
T_CHUNKS = ((0, 32), (32, 32), (64, 32), (96, 48))


def f32(*shape):
    return pltpu.VMEM(shape, F32)


def bf16(*shape):
    return pltpu.VMEM(shape, BF16)


def scratch_of():
    made = dict(
        xf=bf16(R, 1536), tf=bf16(R, 1152), xh=bf16(1536, W), th=bf16(1152, W),
        sums_t=f32(4, 8, 256), sums_i=f32(4, 8, 256), along_t=f32(4, 8, 256), along_i=f32(4, 8, 256),
        norm_t=f32(RT, 128), norm_i=f32(RT, 128), dir_t=f32(RT, W), dir_i=f32(RT, W),
        parts=bf16(2, RI, W), texts_a=bf16(2, 4, RA, 2 * W), texts_b=bf16(2, 4, RB, 2 * W), images=bf16(8, RI, 2 * W),
        mine_a=f32(4, RI, 8 * RA), theirs_a=f32(4, RI, 8 * RA), got_a=f32(4, RI, 8 * RA), pg_a=bf16(8, RI, 8 * RA),
        mine_b=f32(4, RI, 8 * RB), theirs_b=f32(4, RI, 8 * RB), got_b=f32(4, RI, 8 * RB), pg_b=bf16(8, RI, 8 * RB),
        grad_i=f32(8, RI, 2 * W), grad_a=f32(2, 4, RA, 2 * W), grad_b=f32(2, 4, RB, 2 * W),
        grad_as=bf16(2, 4, RA, 2 * W), grad_bs=bf16(2, 4, RB, 2 * W),
        a1=bf16(3, 2, RA, 2 * W), a_sum=f32(2, RA, 2 * W), a_s=bf16(2, RA, 2 * W), a2=bf16(3, RA, W),
        b1=bf16(3, 4, RB, W), b_sum=f32(4, RB, W), b_s=bf16(4, RB, W), b2=bf16(3, RB, W),
        swap_s=bf16(RI, W), swap_r=bf16(RI, W), both=f32(2, RI, W), t_sum=f32(RT, W),
        head_t=f32(1152, W), head_i=f32(1536, W), si=bf16(8, 192, W), ri=bf16(7, 192, W),
        zi=f32(8, 24, W), zi_s=bf16(8, 32, W), zi_r=bf16(7, 32, W), xt=f32(8, 24, W), xt_r=f32(7, 24, W),
    )

    def ring(name, steps, *shapes):
        for q, shape in enumerate(shapes):
            made[f"{name}_s{q}"] = bf16(2, steps, *shape)
            made[f"{name}_r{q}"] = bf16(2, steps, *shape)

    ring("img", 4, *((n, W) for _, (_, n) in I_CHUNKS))
    ring("ht", 4, *((n, W) for _, n in T_CHUNKS))
    made.update(
        send_sem=pltpu.SemaphoreType.DMA((MESSAGES,)),
        recv_sem=pltpu.SemaphoreType.DMA((MESSAGES,)),
        load_sem=pltpu.SemaphoreType.DMA((4,)),
    )
    return made


def kernel(names, xf_any, tf_any, xh_any, th_any, log_temp, logit_bias, out_i, out_t, *refs):
    s = types.SimpleNamespace(**dict(zip(names, refs)))
    dp, mp = lax.axis_index("dp"), lax.axis_index("mp")
    z, xl, y = lax.div(dp, 8), lax.rem(lax.div(dp, 4), 2), lax.rem(dp, 4)
    xh, core = lax.div(mp, 2), lax.rem(mp, 2)
    x = xh * 2 + xl
    slot = xl * 4 + y

    def at(z_at=None, x_at=None, y_at=None, core_at=None):
        z_at = z if z_at is None else z_at
        x_at = x if x_at is None else x_at
        y_at = y if y_at is None else y_at
        core_at = core if core_at is None else core_at
        return (
            (z_at * 2 + lax.rem(x_at, 2)) * 4 + y_at,
            lax.div(x_at, 2) * 2 + core_at,
        )

    def zo(o):
        return lax.rem(z + o + 8, 8)

    def xo(o):
        return lax.rem(x + o + 4, 4)

    def yo(o):
        return lax.rem(y + o + 4, 4)

    def to_z(o):
        return at(z_at=zo(o))

    def to_x(o):
        return at(x_at=xo(o))

    def to_y(o):
        return at(y_at=yo(o))

    across = at(x_at=xh * 2 + 1 - xl)
    twin = at(core_at=1 - core)

    started = []

    def message(src, dst, where):
        k = len(started)
        copy = pltpu.make_async_remote_copy(
            src_ref=src, dst_ref=dst, send_sem=s.send_sem.at[k], recv_sem=s.recv_sem.at[k],
            device_id=where, device_id_type=MESH,
        )
        copy.start()
        started.append(copy)
        return copy

    def lanes(half):
        return pl.ds(pl.multiple_of(half * W, 128), W)

    def rows(span):
        return pl.ds(span[0], span[1])

    def length_of(n, q, way):
        return n // 2 - (q + way) % 2

    def gather(view, to, n):
        flows = {}

        def start(q):
            for way, sign in ((0, 1), (1, -1)):
                flows[way, q, 1] = message(view(0, q), view(0, q), to(sign))

        def advance(step, q):
            for way, sign in ((0, 1), (1, -1)):
                length = length_of(n, q, way)
                if step <= length:
                    flows[way, q, step].wait_recv()
                if step < length:
                    block = view(-sign * step, q)
                    flows[way, q, step + 1] = message(block, block, to(sign))

        return start, advance

    def reduce(name, piece, to, n, finish, count, last_to=None):
        flows = {}

        def buffer(kind, q, way, step):
            return getattr(s, f"{name}_{kind}{q}").at[way, step - 1]

        for step in range(1, n // 2 + 1):
            for q in range(count):
                for way, sign in ((0, 1), (1, -1)):
                    first = n // 2 + 1 - length_of(n, q, way)
                    if step < first:
                        continue
                    value = piece(q, sign * (n // 2 + 1 - step))
                    if step > first:
                        flows[way, q, step - 1].wait_recv()
                        value = value + buffer("r", q, way, step - 1)[...].astype(F32)
                    buffer("s", q, way, step)[...] = value.astype(BF16)
                    where = to(sign) if step < n // 2 or last_to is None else last_to(q, sign)
                    flows[way, q, step] = message(buffer("s", q, way, step), buffer("r", q, way, step), where)
            yield
        for q in range(count):
            total = None
            for way in (0, 1):
                flows[way, q, n // 2].wait_recv()
                value = buffer("r", q, way, n // 2)[...].astype(F32)
                total = value if total is None else total + value
            finish(q, total)
        yield

    barrier = pltpu.get_barrier_semaphore()
    peers = [at(x_at=xo(a), y_at=yo(b)) for a in range(4) for b in range(4) if a or b]
    peers += [to_z(o) for o in range(1, 8)]
    peers += [twin, at(x_at=xo(2), core_at=1 - core)] + [at(z_at=zo(o), x_at=xo(2)) for o in (1, -1)]
    loads = [
        pltpu.make_async_copy(src, dst, s.load_sem.at[k])
        for k, (src, dst) in enumerate(((th_any, s.th), (tf_any, s.tf), (xh_any, s.xh), (xf_any, s.xf)))
    ]
    for copy in loads:
        copy.start()
    for peer in peers:
        pl.semaphore_signal(barrier, inc=1, device_id=peer, device_id_type=MESH)

    def padded(value, count):
        return jnp.concatenate([value, jnp.zeros((count - value.shape[0],) + value.shape[1:], value.dtype)], axis=0)

    def send_sums(ref, value):
        wide = jnp.broadcast_to(jnp.sum(value, axis=1, keepdims=True), (RT, 128))
        ref[mp] = padded(wide, 256).T[0:8]

        def send():
            return [
                message(ref.at[mp], ref.at[mp], where)
                for where in (twin, to_x(2), at(x_at=xo(2), core_at=1 - core))
            ]

        return send

    def sums_of(ref, got):
        for copy in got:
            copy.wait_recv()
        total = (ref[0] + ref[1]) + (ref[2] + ref[3])
        return jnp.broadcast_to(total[0:1], (128, 256)).T[0:RT]

    loads[0].wait()
    loads[1].wait()
    txt_pre = padded(jnp.dot(s.tf[...], s.th[...], preferred_element_type=F32), RT)
    s.dir_t[...] = txt_pre
    send_t = send_sums(s.sums_t, txt_pre * txt_pre)
    pl.semaphore_wait(barrier, len(peers))
    sent_t = send_t()
    loads[2].wait()
    loads[3].wait()
    img_pre = padded(jnp.dot(s.xf[...], s.xh[...], preferred_element_type=F32), RT)
    s.dir_i[...] = img_pre
    sent_i = send_sums(s.sums_i, img_pre * img_pre)()
    norm = jnp.sqrt(sums_of(s.sums_t, sent_t) + 1e-06)
    s.norm_t[...] = norm
    txt_dir = s.dir_t[...] / norm[:, 0:1]
    s.dir_t[...] = txt_dir

    own = lanes(xh)
    kinds = (own, lanes(1 - xh))
    s.texts_a[xl, y, :, own] = txt_dir[0:RA].astype(BF16)
    s.texts_b[xl, y, :, own] = txt_dir[RA:RT].astype(BF16)
    view = s.texts_a.at[xl, y, :, own]
    go_a1 = [message(view, view, to_x(o)) for o in (1, 2, 3)]
    view = s.texts_b.at[xl, y, :, own]
    go_b1 = [message(view, view, to_y(o)) for o in (1, 2, 3)]
    norm = jnp.sqrt(sums_of(s.sums_i, sent_i) + 1e-06)
    s.norm_i[...] = norm
    img_dir = s.dir_i[...] / norm[:, 0:1]
    s.dir_i[...] = img_dir
    s.parts[0] = padded(img_dir[0:64], RI).astype(BF16)
    s.parts[1] = img_dir[64:144].astype(BF16)
    swap = message(s.parts.at[1 - xh], s.images.at[z, :, own], to_x(2))
    s.images[z, :, own] = s.parts[xh]

    def image_chunk(o, q):
        kind, span = I_CHUNKS[q]
        return s.images.at[zo(o), rows(span), kinds[kind]]

    start, advance = gather(image_chunk, to_z, 8)
    start(0)
    start(1)
    swap.wait_recv()
    start(2)
    start(3)
    advance(1, 0)
    advance(1, 1)
    for copy in go_a1:
        copy.wait_recv()
    view = s.texts_a.at[:, y]
    go_a2 = [message(view, view, to_y(o)) for o in (1, 2, 3)]
    for copy in go_b1:
        copy.wait_recv()
    view = s.texts_b.at[xl, :, :, own]
    go_b2 = [message(view, view, to_x(o)) for o in (1, 2, 3)]
    advance(1, 2)
    advance(1, 3)
    for step in (2, 3, 4):
        for q in range(4):
            advance(step, q)

    temper = jnp.exp(jnp.full((1, 128), log_temp[0], F32))[:, 0:1]
    bias = logit_bias[0]
    half = pl.ds(core * 4, 4)

    def products(part, count):
        texts, theirs, got, mine = (getattr(s, f"{k}_{part}") for k in ("texts", "theirs", "got", "mine"))
        columns = texts[...].reshape(8 * count, 2 * W)
        theirs[...] = lax.dot_general(
            s.images[pl.ds((1 - core) * 4, 4)].reshape(4 * RI, 2 * W), columns, NT, preferred_element_type=F32
        ).reshape(4, RI, 8 * count)
        cross = message(theirs, got, twin)
        mine[...] = lax.dot_general(
            s.images[half].reshape(4 * RI, 2 * W), columns, NT, preferred_element_type=F32
        ).reshape(4, RI, 8 * count)
        return cross

    def pairs(part, count, first, cross):
        got, mine, pg = (getattr(s, f"{k}_{part}") for k in ("got", "mine", "pg"))
        shape = (RI, 8 * count)
        ahead = lax.broadcasted_iota(jnp.int32, shape, 1) - lax.broadcasted_iota(jnp.int32, shape, 0)
        column = lax.broadcasted_iota(jnp.int32, (1, 8 * count), 1) - slot * count
        here = (column >= 0) & (column < count)
        cross.wait_recv()

        @pl.loop(0, 4)
        def _(block):
            logits = temper * (mine[block] + got[block]) + bias
            same = here & (ahead == jnp.where(core * 4 + block == z, slot * count + 64 * xh - first, -8192))
            pg[core * 4 + block] = (temper * (jax.nn.sigmoid(logits) - same.astype(F32))).astype(BF16)

        return message(pg.at[half], pg.at[half], twin)

    def text_grads(part, count):
        pg, grad, grad_s = (getattr(s, k) for k in (f"pg_{part}", f"grad_{part}", f"grad_{part}s"))
        value = lax.dot_general(
            pg[...].reshape(8 * RI, 8 * count), s.images[...].reshape(8 * RI, 2 * W), TN, preferred_element_type=F32
        ).reshape(2, 4, count, 2 * W)
        grad[...] = value
        grad_s[...] = value.astype(BF16)

    for copy in go_a2:
        copy.wait_recv()
    cross_a = products("a", RA)
    share_a = pairs("a", RA, 0, cross_a)
    for copy in go_b2:
        copy.wait_recv()
    cross_b = products("b", RB)
    share_a.wait_recv()
    text_grads("a", RA)
    back_a1 = [message(s.grad_as.at[:, yo(o)], s.a1.at[o - 1], to_y(o)) for o in (1, 2, 3)]
    share_b = pairs("b", RB, RA, cross_b)
    s.grad_i[...] = lax.dot_general(
        s.pg_a[...].reshape(8 * RI, 8 * RA), s.texts_a[...].reshape(8 * RA, 2 * W), NN, preferred_element_type=F32
    ).reshape(8, RI, 2 * W)
    share_b.wait_recv()
    text_grads("b", RB)
    back_b1 = [
        message(s.grad_bs.at[lax.rem(xo(o), 2), :, :, lanes(lax.div(xo(o), 2))], s.b1.at[o - 1], to_x(o))
        for o in (1, 2, 3)
    ]
    s.grad_i[...] += lax.dot_general(
        s.pg_b[...].reshape(8 * RI, 8 * RB), s.texts_b[...].reshape(8 * RB, 2 * W), NN, preferred_element_type=F32
    ).reshape(8, RI, 2 * W)

    def image_term(q, o):
        kind, span = I_CHUNKS[q]
        return s.grad_i[zo(o), rows(span), kinds[kind]]

    def image_done(q, total):
        kind, span = I_CHUNKS[q]
        if kind == 0:
            s.both[xh, rows(span)] = total + image_term(q, 0)
        else:
            s.both[1 - xh, rows(span)] = total

    back_z = reduce(
        "img", image_term, to_z, 8, image_done, 4,
        lambda q, sign: to_z(sign) if I_CHUNKS[q][0] == 0 else at(z_at=zo(sign), x_at=xo(2)),
    )
    next(back_z)
    s.swap_s[...] = s.grad_i[z, :, kinds[1]].astype(BF16)
    swap_back = message(s.swap_s, s.swap_r, to_x(2))
    next(back_z)
    next(back_z)
    for copy in back_a1:
        copy.wait_recv()
    s.a_sum[...] = s.grad_a[:, y] + sum(s.a1[o].astype(F32) for o in range(3))
    s.a_s[...] = s.a_sum[...].astype(BF16)
    back_a2 = [
        message(s.a_s.at[lax.rem(xo(o), 2), :, lanes(lax.div(xo(o), 2))], s.a2.at[o - 1], to_x(o)) for o in (1, 2, 3)
    ]
    next(back_z)
    for copy in back_b1:
        copy.wait_recv()
    s.b_sum[...] = s.grad_b[xl, :, :, own] + sum(s.b1[o].astype(F32) for o in range(3))
    s.b_s[...] = s.b_sum[...].astype(BF16)
    back_b2 = [message(s.b_s.at[yo(o)], s.b2.at[o - 1], to_y(o)) for o in (1, 2, 3)]
    next(back_z)
    swap_back.wait_recv()
    s.both[1 - xh] += s.swap_r[...].astype(F32)
    img_unit_grad = jnp.concatenate([s.both[0, pl.ds(0, 64)], s.both[1]], axis=0)
    sent_i = send_sums(s.along_i, img_unit_grad * s.dir_i[...])()
    for copy in back_a2:
        copy.wait_recv()
    s.t_sum[pl.ds(0, RA)] = s.a_sum[xl, :, own] + sum(s.a2[o].astype(F32) for o in range(3))
    for copy in back_b2:
        copy.wait_recv()
    s.t_sum[pl.ds(RA, RB)] = s.b_sum[y] + sum(s.b2[o].astype(F32) for o in range(3))
    sent_t = send_sums(s.along_t, s.t_sum[...] * s.dir_t[...])()

    along = sums_of(s.along_i, sent_i)
    img_unit_grad = jnp.concatenate([s.both[0, pl.ds(0, 64)], s.both[1]], axis=0)
    img_grad = ((img_unit_grad - s.dir_i[...] * along[:, 0:1]) / s.norm_i[:, 0:1]).astype(BF16)
    s.head_i[...] = lax.dot_general(s.xf[...], img_grad[0:R], TN, preferred_element_type=F32)
    for j in range(8):
        s.si[j] = jnp.concatenate([s.head_i[pl.ds(k * 192 + j * 24, 24), :] for k in range(8)], axis=0).astype(BF16)

    def over_xy(src, dst):
        copies = []
        for a in (1, 0):
            for b in (2, 1, 3, 0):
                if a or b:
                    to_xl = lax.rem(xl + a, 2)
                    where = at(x_at=xh * 2 + to_xl, y_at=yo(b))
                    copies.append(message(src.at[to_xl * 4 + yo(b)], dst.at[a * 4 + b - 1], where))
        return copies

    fore_i = over_xy(s.si, s.ri)
    along = sums_of(s.along_t, sent_t)
    txt_grad = ((s.t_sum[...] - s.dir_t[...] * along[:, 0:1]) / s.norm_t[:, 0:1]).astype(BF16)
    s.head_t[...] = lax.dot_general(s.tf[...], txt_grad[0:R], TN, preferred_element_type=F32)

    def text_term(q, o):
        return s.head_t[pl.ds(pl.multiple_of(zo(o) * RT + T_CHUNKS[q][0], 16), T_CHUNKS[q][1]), :]

    def text_done(q, total):
        s.t_sum[rows(T_CHUNKS[q])] = total + text_term(q, 0)

    fore_t = reduce("ht", text_term, to_z, 8, text_done, 4)
    next(fore_t)
    next(fore_t)
    next(fore_t)
    next(fore_t)
    for copy in fore_i:
        copy.wait_recv()
    for k in range(8):
        s.zi[k] = s.head_i[pl.ds(pl.multiple_of(k * 192 + slot * 24, 8), 24), :]
    s.zi[...] += sum(s.ri[j].astype(F32) for j in range(7)).reshape(8, 24, W)
    for k in range(8):
        s.zi_s[k] = padded(s.zi[k], 32).astype(BF16)
    last_i = [message(s.zi_s.at[zo(o)], s.zi_r.at[o - 1], to_z(o)) for o in (4, 3, 5, 2, 6, 1, 7)]
    next(fore_t)
    total = s.t_sum[...]
    for j in range(8):
        s.xt[j] = padded(total[18 * j : 18 * j + 18], 24)
    last_t = over_xy(s.xt, s.xt_r)
    for copy in last_t:
        copy.wait_recv()
    out_t[...] = (s.xt[slot] + sum(s.xt_r[j] for j in range(7)))[0:18]
    for copy in last_i:
        copy.wait_recv()
    out_i[...] = s.zi[z] + sum(s.zi_r[j].astype(F32) for j in range(7))[0:24]
    for copy in started:
        copy.wait_send()


def body(image_feats, text_feats, image_head, text_head, log_temp, logit_bias):
    vmem = pl.BlockSpec(memory_space=pltpu.VMEM)
    smem = pl.BlockSpec(memory_space=pltpu.SMEM)
    anywhere = pl.BlockSpec(memory_space=pl.ANY)
    scratch = scratch_of()

    def run(*refs):
        kernel(tuple(scratch), *refs)

    return pl.pallas_call(
        run,
        out_shape=(jax.ShapeDtypeStruct((24, W), F32), jax.ShapeDtypeStruct((18, W), F32)),
        in_specs=[anywhere, anywhere, anywhere, anywhere, smem, smem],
        out_specs=(vmem, vmem),
        scratch_shapes=list(scratch.values()),
        compiler_params=pltpu.CompilerParams(
            collective_id=0, has_side_effects=True, vmem_limit_bytes=56 * 1024 * 1024
        ),
        name="pair_loss",
    )(image_feats, text_feats, image_head, text_head, log_temp, logit_bias)


def solution(mesh):
    placed = (P("dp", None), P("dp", None), P(None, "mp"), P(None, "mp"), P(), P())
    return jax.shard_map(
        body, mesh=mesh, in_specs=placed, out_specs=(P("dp", "mp"), P("dp", "mp")), check_vma=False
    )
```

```python
import types

import jax
import jax.numpy as jnp
from jax import lax
from jax.experimental import pallas as pl
from jax.experimental.pallas import tpu as pltpu
from jax.sharding import PartitionSpec as P

F32 = jnp.float32
BF16 = jnp.bfloat16
MESH = pl.DeviceIdType.MESH
NT = (((1,), (1,)), ((), ()))
TN = (((0,), (0,)), ((), ()))
NN = (((1,), (0,)), ((), ()))
R = 136
RT = 144
RI = 80
W = 384
MESSAGES = 200
RA, RB = 64, 80
I_CHUNKS = ((0, (0, 48)), (0, (48, 32)), (1, (0, 48)), (1, (48, 32)))
T_CHUNKS = ((0, 32), (32, 32), (64, 32), (96, 48))


def f32(*shape):
    return pltpu.VMEM(shape, F32)


def bf16(*shape):
    return pltpu.VMEM(shape, BF16)


def scratch_of():
    made = dict(
        xf=bf16(R, 1536), tf=bf16(R, 1152), xh=bf16(1536, W), th=bf16(1152, W),
        texts_an=bf16(2, 4, RA, 2 * W), texts_bn=bf16(2, 4, RB, 2 * W), images_n=bf16(8, RI, 2 * W),
        all_t=f32(8, 8, 256), all_i=f32(8, 8, 256), columns_t=f32(256, 128), columns_i=f32(256, 128),
        sums_t=f32(4, 8, 256), sums_i=f32(4, 8, 256), along_t=f32(4, 8, 256), along_i=f32(4, 8, 256),
        norm_t=f32(RT, 128), norm_i=f32(RT, 128), dir_t=f32(RT, W), dir_i=f32(RT, W),
        parts=bf16(2, RI, W), texts_a=bf16(2, 4, RA, 2 * W), texts_b=bf16(2, 4, RB, 2 * W), images=bf16(8, RI, 2 * W),
        mine_a=f32(4, RI, 8 * RA), theirs_a=f32(4, RI, 8 * RA), got_a=f32(4, RI, 8 * RA), pg_a=bf16(8, RI, 8 * RA),
        mine_b=f32(4, RI, 8 * RB), theirs_b=f32(4, RI, 8 * RB), got_b=f32(4, RI, 8 * RB), pg_b=bf16(8, RI, 8 * RB),
        grad_i=f32(8, RI, 2 * W), grad_a=f32(2, 4, RA, 2 * W), grad_b=f32(2, 4, RB, 2 * W),
        grad_as=bf16(2, 4, RA, 2 * W), grad_bs=bf16(2, 4, RB, 2 * W),
        a1=bf16(3, 2, RA, 2 * W), a_sum=f32(2, RA, 2 * W), a_s=bf16(2, RA, 2 * W), a2=bf16(3, RA, W),
        b1=bf16(3, 4, RB, W), b_sum=f32(4, RB, W), b_s=bf16(4, RB, W), b2=bf16(3, RB, W),
        swap_s=bf16(RI, W), swap_r=bf16(RI, W), both=f32(2, RI, W), t_sum=f32(RT, W),
        head_t=f32(1152, W), head_i=f32(1536, W), si=bf16(8, 192, W), ri=bf16(7, 192, W),
        zi=f32(8, 24, W), zi_s=bf16(8, 32, W), zi_r=bf16(7, 32, W), xt=f32(8, 24, W), xt_r=f32(7, 24, W),
    )

    def ring(name, steps, *shapes):
        for q, shape in enumerate(shapes):
            made[f"{name}_s{q}"] = bf16(2, steps, *shape)
            made[f"{name}_r{q}"] = bf16(2, steps, *shape)

    ring("img", 4, *((n, W) for _, (_, n) in I_CHUNKS))
    ring("ht", 4, *((n, W) for _, n in T_CHUNKS))
    made.update(
        send_sem=pltpu.SemaphoreType.DMA((MESSAGES,)),
        recv_sem=pltpu.SemaphoreType.DMA((MESSAGES,)),
        load_sem=pltpu.SemaphoreType.DMA((4,)),
    )
    return made


def kernel(names, xf_any, tf_any, xh_any, th_any, log_temp, logit_bias, out_i, out_t, *refs):
    s = types.SimpleNamespace(**dict(zip(names, refs)))
    dp, mp = lax.axis_index("dp"), lax.axis_index("mp")
    z, xl, y = lax.div(dp, 8), lax.rem(lax.div(dp, 4), 2), lax.rem(dp, 4)
    xh, core = lax.div(mp, 2), lax.rem(mp, 2)
    x = xh * 2 + xl
    slot = xl * 4 + y

    def at(z_at=None, x_at=None, y_at=None, core_at=None):
        z_at = z if z_at is None else z_at
        x_at = x if x_at is None else x_at
        y_at = y if y_at is None else y_at
        core_at = core if core_at is None else core_at
        return (
            (z_at * 2 + lax.rem(x_at, 2)) * 4 + y_at,
            lax.div(x_at, 2) * 2 + core_at,
        )

    def zo(o):
        return lax.rem(z + o + 8, 8)

    def xo(o):
        return lax.rem(x + o + 4, 4)

    def yo(o):
        return lax.rem(y + o + 4, 4)

    def to_z(o):
        return at(z_at=zo(o))

    def to_x(o):
        return at(x_at=xo(o))

    def to_y(o):
        return at(y_at=yo(o))

    across = at(x_at=xh * 2 + 1 - xl)
    twin = at(core_at=1 - core)

    started = []

    def message(src, dst, where):
        k = len(started)
        copy = pltpu.make_async_remote_copy(
            src_ref=src, dst_ref=dst, send_sem=s.send_sem.at[k], recv_sem=s.recv_sem.at[k],
            device_id=where, device_id_type=MESH,
        )
        copy.start()
        started.append(copy)
        return copy

    flushed = [0]

    def flush(upto):
        for copy in started[flushed[0] : upto]:
            copy.wait_send()
        flushed[0] = max(upto, flushed[0])

    def lanes(half):
        return pl.ds(pl.multiple_of(half * W, 128), W)

    def rows(span):
        return pl.ds(span[0], span[1])

    def length_of(n, q, way):
        return n // 2 - (q + way) % 2

    def gather(view, to, n):
        flows = {}

        def start(q):
            for way, sign in ((0, 1), (1, -1)):
                flows[way, q, 1] = message(view(0, q), view(0, q), to(sign))

        def advance(step, q):
            for way, sign in ((0, 1), (1, -1)):
                length = length_of(n, q, way)
                if step <= length:
                    flows[way, q, step].wait_recv()
                if step < length:
                    block = view(-sign * step, q)
                    flows[way, q, step + 1] = message(block, block, to(sign))

        return start, advance

    def reduce(name, piece, to, n, finish, count, last_to=None):
        flows = {}

        def buffer(kind, q, way, step):
            return getattr(s, f"{name}_{kind}{q}").at[way, step - 1]

        for step in range(1, n // 2 + 1):
            for q in range(count):
                for way, sign in ((0, 1), (1, -1)):
                    first = n // 2 + 1 - length_of(n, q, way)
                    if step < first:
                        continue
                    value = piece(q, sign * (n // 2 + 1 - step))
                    if step > first:
                        flows[way, q, step - 1].wait_recv()
                        value = value + buffer("r", q, way, step - 1)[...].astype(F32)
                    buffer("s", q, way, step)[...] = value.astype(BF16)
                    where = to(sign) if step < n // 2 or last_to is None else last_to(q, sign)
                    flows[way, q, step] = message(buffer("s", q, way, step), buffer("r", q, way, step), where)
            yield
        for q in range(count):
            total = None
            for way in (0, 1):
                flows[way, q, n // 2].wait_recv()
                value = buffer("r", q, way, n // 2)[...].astype(F32)
                total = value if total is None else total + value
            finish(q, total)
        yield

    barrier = pltpu.get_barrier_semaphore()
    peers = [at(x_at=xo(a), y_at=yo(b)) for a in range(4) for b in range(4) if a or b]
    peers += [to_z(o) for o in range(1, 8)]
    peers += [twin, at(x_at=xo(2), core_at=1 - core)] + [at(z_at=zo(o), x_at=xo(2)) for o in (1, -1)]
    loads = [
        pltpu.make_async_copy(src, dst, s.load_sem.at[k])
        for k, (src, dst) in enumerate(((th_any, s.th), (tf_any, s.tf), (xh_any, s.xh), (xf_any, s.xf)))
    ]
    for copy in loads:
        copy.start()
    for peer in peers:
        pl.semaphore_signal(barrier, inc=1, device_id=peer, device_id_type=MESH)

    def padded(value, count):
        return jnp.concatenate([value, jnp.zeros((count - value.shape[0],) + value.shape[1:], value.dtype)], axis=0)

    def send_sums(ref, value):
        wide = jnp.broadcast_to(jnp.sum(value, axis=1, keepdims=True), (RT, 128))
        ref[mp] = padded(wide, 256).T[0:8]

        def send():
            return [
                message(ref.at[mp], ref.at[mp], where)
                for where in (twin, to_x(2), at(x_at=xo(2), core_at=1 - core))
            ]

        return send

    def sums_of(ref, got):
        for copy in got:
            copy.wait_recv()
        return (ref[0] + ref[1]) + (ref[2] + ref[3])

    def down(total):
        return jnp.broadcast_to(total[0:1], (128, 256)).T[0:RT]

    def over_xy(src, dst, place=None):
        copies = []
        for a in (1, 0):
            for b in (2, 1, 3, 0):
                if a or b:
                    to_xl = lax.rem(xl + a, 2)
                    where = at(x_at=xh * 2 + to_xl, y_at=yo(b))
                    if place is None:
                        copies.append(message(src.at[to_xl * 4 + yo(b)], dst.at[a * 4 + b - 1], where))
                    else:
                        copies.append(message(src.at[place], dst.at[place], where))
        return copies

    loads[0].wait()
    loads[1].wait()
    txt_pre = padded(jnp.dot(s.tf[...], s.th[...], preferred_element_type=F32), RT)
    s.dir_t[...] = txt_pre
    send_t = send_sums(s.sums_t, txt_pre * txt_pre)
    own = lanes(xh)
    kinds = (own, lanes(1 - xh))
    s.texts_a[xl, y, :, own] = txt_pre[0:RA].astype(BF16)
    s.texts_b[xl, y, :, own] = txt_pre[RA:RT].astype(BF16)
    pl.semaphore_wait(barrier, len(peers))

    sent_t = send_t()
    view = s.texts_a.at[xl, y, :, own]
    go_a1 = [message(view, view, to_x(o)) for o in (1, 2, 3)]
    view = s.texts_b.at[xl, y, :, own]
    go_b1 = [message(view, view, to_y(o)) for o in (1, 2, 3)]
    loads[2].wait()
    loads[3].wait()
    img_pre = padded(jnp.dot(s.xf[...], s.xh[...], preferred_element_type=F32), RT)
    s.dir_i[...] = img_pre
    s.parts[0] = padded(img_pre[0:64], RI).astype(BF16)
    s.parts[1] = img_pre[64:144].astype(BF16)
    swap = message(s.parts.at[1 - xh], s.images.at[z, :, own], to_x(2))
    s.images[z, :, own] = s.parts[xh]

    def image_chunk(o, q):
        kind, span = I_CHUNKS[q]
        return s.images.at[zo(o), rows(span), kinds[kind]]

    start, advance = gather(image_chunk, to_z, 8)
    start(0)
    start(1)
    sent_i = send_sums(s.sums_i, img_pre * img_pre)()
    s.all_t[slot] = sums_of(s.sums_t, sent_t)
    norms_t = over_xy(s.all_t, s.all_t, slot)
    swap.wait_recv()
    start(2)
    start(3)
    advance(1, 0)
    advance(1, 1)
    for copy in go_a1:
        copy.wait_recv()
    view = s.texts_a.at[:, y]
    go_a2 = [message(view, view, to_y(o)) for o in (1, 2, 3)]
    for copy in go_b1:
        copy.wait_recv()
    view = s.texts_b.at[xl, :, :, own]
    go_b2 = [message(view, view, to_x(o)) for o in (1, 2, 3)]
    s.all_i[z] = sums_of(s.sums_i, sent_i)
    norms_i = [message(s.all_i.at[z], s.all_i.at[z], to_z(o)) for o in range(1, 8)]
    advance(1, 2)
    advance(1, 3)
    for name, place in (("t", slot), ("i", z)):
        norm = jnp.sqrt(down(getattr(s, f"all_{name}")[place]) + 1e-06)
        getattr(s, f"norm_{name}")[...] = norm
        side = getattr(s, f"dir_{name}")
        side[...] = side[...] / norm[:, 0:1]
    for q in range(4):
        advance(2, q)

    def columns_of(name, copies):
        for copy in copies:
            copy.wait_recv()
        every = getattr(s, f"all_{name}")
        sums = jnp.concatenate([every[k, 0:1] for k in range(8)], axis=0)
        getattr(s, f"columns_{name}")[...] = padded(1.0 / jnp.sqrt(sums + 1e-06), 128).T

    columns_of("t", norms_t)
    for q in range(4):
        advance(3, q)
    columns_of("i", norms_i)
    for q in range(4):
        advance(4, q)
    for k in range(8):
        s.images_n[k] = (s.images[k].astype(F32) * s.columns_i[pl.ds(pl.multiple_of(xh * 64, 8), RI), k : k + 1]).astype(BF16)

    def text_units(part, first, count, copies):
        for copy in copies:
            copy.wait_recv()
        texts, units = getattr(s, f"texts_{part}"), getattr(s, f"texts_{part}n")
        for k in range(8):
            units[k // 4, k % 4] = (
                texts[k // 4, k % 4].astype(F32) * s.columns_t[pl.ds(first, count), k : k + 1]
            ).astype(BF16)

    temper = jnp.exp(jnp.full((1, 128), log_temp[0], F32))[:, 0:1]
    bias = logit_bias[0]
    half = pl.ds(core * 4, 4)

    def products(part, count):
        texts, theirs, got, mine = (
            getattr(s, k) for k in (f"texts_{part}n", f"theirs_{part}", f"got_{part}", f"mine_{part}")
        )
        columns = texts[...].reshape(8 * count, 2 * W)
        theirs[...] = lax.dot_general(
            s.images_n[pl.ds((1 - core) * 4, 4)].reshape(4 * RI, 2 * W), columns, NT, preferred_element_type=F32
        ).reshape(4, RI, 8 * count)
        cross = message(theirs, got, twin)
        mine[...] = lax.dot_general(
            s.images_n[half].reshape(4 * RI, 2 * W), columns, NT, preferred_element_type=F32
        ).reshape(4, RI, 8 * count)
        return cross

    def pairs(part, count, first, cross):
        got, mine, pg = (getattr(s, f"{k}_{part}") for k in ("got", "mine", "pg"))
        shape = (RI, 8 * count)
        ahead = lax.broadcasted_iota(jnp.int32, shape, 1) - lax.broadcasted_iota(jnp.int32, shape, 0)
        column = lax.broadcasted_iota(jnp.int32, (1, 8 * count), 1) - slot * count
        here = (column >= 0) & (column < count)
        cross.wait_recv()

        @pl.loop(0, 4)
        def _(block):
            logits = temper * (mine[block] + got[block]) + bias
            same = here & (ahead == jnp.where(core * 4 + block == z, slot * count + 64 * xh - first, -8192))
            pg[core * 4 + block] = (temper * (jax.nn.sigmoid(logits) - same.astype(F32))).astype(BF16)

        return message(pg.at[half], pg.at[half], twin)

    def text_grads(part, count):
        pg, grad, grad_s = (getattr(s, k) for k in (f"pg_{part}", f"grad_{part}", f"grad_{part}s"))
        value = lax.dot_general(
            pg[...].reshape(8 * RI, 8 * count), s.images_n[...].reshape(8 * RI, 2 * W), TN, preferred_element_type=F32
        ).reshape(2, 4, count, 2 * W)
        grad[...] = value
        grad_s[...] = value.astype(BF16)

    text_units("a", 0, RA, go_a2)
    cross_a = products("a", RA)
    share_a = pairs("a", RA, 0, cross_a)
    text_units("b", RA, RB, go_b2)
    arrived = len(started)
    cross_b = products("b", RB)
    share_a.wait_recv()
    text_grads("a", RA)
    back_a1 = [message(s.grad_as.at[:, yo(o)], s.a1.at[o - 1], to_y(o)) for o in (1, 2, 3)]
    share_b = pairs("b", RB, RA, cross_b)
    s.grad_i[...] = lax.dot_general(
        s.pg_a[...].reshape(8 * RI, 8 * RA), s.texts_an[...].reshape(8 * RA, 2 * W), NN, preferred_element_type=F32
    ).reshape(8, RI, 2 * W)
    share_b.wait_recv()
    text_grads("b", RB)
    back_b1 = [
        message(s.grad_bs.at[lax.rem(xo(o), 2), :, :, lanes(lax.div(xo(o), 2))], s.b1.at[o - 1], to_x(o))
        for o in (1, 2, 3)
    ]
    s.grad_i[...] += lax.dot_general(
        s.pg_b[...].reshape(8 * RI, 8 * RB), s.texts_bn[...].reshape(8 * RB, 2 * W), NN, preferred_element_type=F32
    ).reshape(8, RI, 2 * W)

    def image_term(q, o):
        kind, span = I_CHUNKS[q]
        return s.grad_i[zo(o), rows(span), kinds[kind]]

    def image_done(q, total):
        kind, span = I_CHUNKS[q]
        if kind == 0:
            s.both[xh, rows(span)] = total + image_term(q, 0)
        else:
            s.both[1 - xh, rows(span)] = total

    back_z = reduce(
        "img", image_term, to_z, 8, image_done, 4,
        lambda q, sign: to_z(sign) if I_CHUNKS[q][0] == 0 else at(z_at=zo(sign), x_at=xo(2)),
    )
    next(back_z)
    s.swap_s[...] = s.grad_i[z, :, kinds[1]].astype(BF16)
    swap_back = message(s.swap_s, s.swap_r, to_x(2))
    flush(arrived)
    next(back_z)
    next(back_z)
    for copy in back_a1:
        copy.wait_recv()
    s.a_sum[...] = s.grad_a[:, y] + sum(s.a1[o].astype(F32) for o in range(3))
    s.a_s[...] = s.a_sum[...].astype(BF16)
    back_a2 = [
        message(s.a_s.at[lax.rem(xo(o), 2), :, lanes(lax.div(xo(o), 2))], s.a2.at[o - 1], to_x(o)) for o in (1, 2, 3)
    ]
    next(back_z)
    for copy in back_b1:
        copy.wait_recv()
    s.b_sum[...] = s.grad_b[xl, :, :, own] + sum(s.b1[o].astype(F32) for o in range(3))
    s.b_s[...] = s.b_sum[...].astype(BF16)
    back_b2 = [message(s.b_s.at[yo(o)], s.b2.at[o - 1], to_y(o)) for o in (1, 2, 3)]
    next(back_z)
    swap_back.wait_recv()
    s.both[1 - xh] += s.swap_r[...].astype(F32)
    img_unit_grad = jnp.concatenate([s.both[0, pl.ds(0, 64)], s.both[1]], axis=0)
    returned = len(started)
    sent_i = send_sums(s.along_i, img_unit_grad * s.dir_i[...])()
    for copy in back_a2:
        copy.wait_recv()
    s.t_sum[pl.ds(0, RA)] = s.a_sum[xl, :, own] + sum(s.a2[o].astype(F32) for o in range(3))
    for copy in back_b2:
        copy.wait_recv()
    s.t_sum[pl.ds(RA, RB)] = s.b_sum[y] + sum(s.b2[o].astype(F32) for o in range(3))
    sent_t = send_sums(s.along_t, s.t_sum[...] * s.dir_t[...])()

    along = down(sums_of(s.along_i, sent_i))
    img_unit_grad = jnp.concatenate([s.both[0, pl.ds(0, 64)], s.both[1]], axis=0)
    img_grad = ((img_unit_grad - s.dir_i[...] * along[:, 0:1]) / s.norm_i[:, 0:1]).astype(BF16)
    s.head_i[...] = lax.dot_general(s.xf[...], img_grad[0:R], TN, preferred_element_type=F32)
    for j in range(8):
        s.si[j] = jnp.concatenate([s.head_i[pl.ds(k * 192 + j * 24, 24), :] for k in range(8)], axis=0).astype(BF16)

    fore_i = over_xy(s.si, s.ri)
    along = down(sums_of(s.along_t, sent_t))
    txt_grad = ((s.t_sum[...] - s.dir_t[...] * along[:, 0:1]) / s.norm_t[:, 0:1]).astype(BF16)
    s.head_t[...] = lax.dot_general(s.tf[...], txt_grad[0:R], TN, preferred_element_type=F32)

    def text_term(q, o):
        return s.head_t[pl.ds(pl.multiple_of(zo(o) * RT + T_CHUNKS[q][0], 16), T_CHUNKS[q][1]), :]

    def text_done(q, total):
        s.t_sum[rows(T_CHUNKS[q])] = total + text_term(q, 0)

    fore_t = reduce("ht", text_term, to_z, 8, text_done, 4)
    next(fore_t)
    flush(returned)
    next(fore_t)
    next(fore_t)
    next(fore_t)
    for copy in fore_i:
        copy.wait_recv()
    for k in range(8):
        s.zi[k] = s.head_i[pl.ds(pl.multiple_of(k * 192 + slot * 24, 8), 24), :]
    s.zi[...] += sum(s.ri[j].astype(F32) for j in range(7)).reshape(8, 24, W)
    for k in range(8):
        s.zi_s[k] = padded(s.zi[k], 32).astype(BF16)
    last_i = [message(s.zi_s.at[zo(o)], s.zi_r.at[o - 1], to_z(o)) for o in (4, 3, 5, 2, 6, 1, 7)]
    next(fore_t)
    total = s.t_sum[...]
    for j in range(8):
        s.xt[j] = padded(total[18 * j : 18 * j + 18], 24)
    before = len(started)
    last_t = over_xy(s.xt, s.xt_r)
    flush(before)
    for copy in last_t:
        copy.wait_recv()
    out_t[...] = (s.xt[slot] + sum(s.xt_r[j] for j in range(7)))[0:18]
    for copy in last_i:
        copy.wait_recv()
    out_i[...] = s.zi[z] + sum(s.zi_r[j].astype(F32) for j in range(7))[0:24]
    flush(len(started))


def body(image_feats, text_feats, image_head, text_head, log_temp, logit_bias):
    vmem = pl.BlockSpec(memory_space=pltpu.VMEM)
    smem = pl.BlockSpec(memory_space=pltpu.SMEM)
    anywhere = pl.BlockSpec(memory_space=pl.ANY)
    scratch = scratch_of()

    def run(*refs):
        kernel(tuple(scratch), *refs)

    found = pl.pallas_call(
        run,
        out_shape=(jax.ShapeDtypeStruct((24, W), F32), jax.ShapeDtypeStruct((18, W), F32)),
        in_specs=[anywhere, anywhere, anywhere, anywhere, smem, smem],
        out_specs=(vmem, vmem),
        scratch_shapes=list(scratch.values()),
        compiler_params=pltpu.CompilerParams(
            collective_id=0, has_side_effects=True, vmem_limit_bytes=56 * 1024 * 1024
        ),
        name="pair_loss",
    )(image_feats, text_feats, image_head, text_head, log_temp, logit_bias)

    def hand_over(a, b, c, d):
        c[...] = a[...]
        d[...] = b[...]

    return pl.pallas_call(
        hand_over,
        out_shape=(jax.ShapeDtypeStruct((24, W), F32), jax.ShapeDtypeStruct((18, W), F32)),
        in_specs=[vmem, vmem],
        out_specs=(vmem, vmem),
        name="hand_over",
    )(*found)


def solution(mesh):
    placed = (P("dp", None), P("dp", None), P(None, "mp"), P(None, "mp"), P(), P())
    return jax.shard_map(
        body, mesh=mesh, in_specs=placed, out_specs=(P("dp", "mp"), P("dp", "mp")), check_vma=False
    )
```

```python
import types

import jax
import jax.numpy as jnp
from jax import lax
from jax.experimental import pallas as pl
from jax.experimental.pallas import tpu as pltpu
from jax.sharding import PartitionSpec as P

F32 = jnp.float32
BF16 = jnp.bfloat16
MESH = pl.DeviceIdType.MESH
NT = (((1,), (1,)), ((), ()))
TN = (((0,), (0,)), ((), ()))
NN = (((1,), (0,)), ((), ()))
R = 136
RT = 144
RI = 80
W = 384
MESSAGES = 200
RA, RB = 80, 64
I_CHUNKS = ((0, (0, 48)), (0, (48, 32)), (1, (0, 48)), (1, (48, 32)))
T_CHUNKS = ((0, 32), (32, 32), (64, 32), (96, 48))


def f32(*shape):
    return pltpu.VMEM(shape, F32)


def bf16(*shape):
    return pltpu.VMEM(shape, BF16)


def scratch_of():
    made = dict(
        xf=bf16(R, 1536), tf=bf16(R, 1152), xh=bf16(1536, W), th=bf16(1152, W),
        texts_an=bf16(2, 4, RA, 2 * W), texts_bn=bf16(2, 4, RB, 2 * W), images_n=bf16(8, RI, 2 * W),
        all_t=f32(8, 8, 256), all_i=f32(8, 8, 256), columns_t=f32(256, 128), columns_i=f32(256, 128),
        sums_t=f32(4, 8, 256), sums_i=f32(4, 8, 256), along_t=f32(4, 8, 256), along_i=f32(4, 8, 256),
        norm_t=f32(RT, 128), norm_i=f32(RT, 128), dir_t=f32(RT, W), dir_i=f32(RT, W),
        parts=bf16(2, RI, W), texts_a=bf16(2, 4, RA, 2 * W), texts_b=bf16(2, 4, RB, 2 * W), images=bf16(8, RI, 2 * W),
        mine_a=f32(4, RI, 8 * RA), theirs_a=f32(4, RI, 8 * RA), got_a=f32(4, RI, 8 * RA), pg_a=bf16(8, RI, 8 * RA),
        mine_b=f32(4, RI, 8 * RB), theirs_b=f32(4, RI, 8 * RB), got_b=f32(4, RI, 8 * RB), pg_b=bf16(8, RI, 8 * RB),
        grad_i=f32(8, RI, 2 * W), grad_a=f32(2, 4, RA, 2 * W), grad_b=f32(2, 4, RB, 2 * W),
        grad_as=bf16(2, 4, RA, 2 * W), grad_bs=bf16(2, 4, RB, 2 * W),
        a1=bf16(3, 2, RA, 2 * W), a_sum=f32(2, RA, 2 * W), a_s=bf16(2, RA, 2 * W), a2=bf16(3, RA, W),
        b1=bf16(3, 4, RB, W), b_sum=f32(4, RB, W), b_s=bf16(4, RB, W), b2=bf16(3, RB, W),
        swap_s=bf16(RI, W), swap_r=bf16(RI, W), both=f32(2, RI, W), t_sum=f32(RT, W),
        head_t=f32(1152, W), head_i=f32(1536, W), si0=bf16(8, 192, 256), ri0=bf16(7, 192, 256), si1=bf16(8, 192, 128), ri1=bf16(7, 192, 128),
        zi=f32(8, 24, W), zi_s0=bf16(8, 32, 256), zi_r0=bf16(7, 32, 256), zi_s1=bf16(8, 32, 128), zi_r1=bf16(7, 32, 128), xt=f32(8, 24, W), xt_r=f32(7, 24, W),
    )

    def ring(name, steps, *shapes):
        for q, shape in enumerate(shapes):
            made[f"{name}_s{q}"] = bf16(2, steps, *shape)
            made[f"{name}_r{q}"] = bf16(2, steps, *shape)

    ring("img", 4, *((n, W) for _, (_, n) in I_CHUNKS))
    ring("ht", 4, *((n, W) for _, n in T_CHUNKS))
    made.update(
        send_sem=pltpu.SemaphoreType.DMA((MESSAGES,)),
        recv_sem=pltpu.SemaphoreType.DMA((MESSAGES,)),
        load_sem=pltpu.SemaphoreType.DMA((6,)),
        scale=pltpu.SMEM((1,), F32), bias=pltpu.SMEM((1,), F32),
    )
    return made


def kernel(names, xf_any, tf_any, xh_any, th_any, log_temp, logit_bias, out_i, out_t, *refs):
    s = types.SimpleNamespace(**dict(zip(names, refs)))
    dp, mp = lax.axis_index("dp"), lax.axis_index("mp")
    z, xl, y = lax.div(dp, 8), lax.rem(lax.div(dp, 4), 2), lax.rem(dp, 4)
    xh, core = lax.div(mp, 2), lax.rem(mp, 2)
    x = xh * 2 + xl
    slot = xl * 4 + y

    def at(z_at=None, x_at=None, y_at=None, core_at=None):
        z_at = z if z_at is None else z_at
        x_at = x if x_at is None else x_at
        y_at = y if y_at is None else y_at
        core_at = core if core_at is None else core_at
        return (
            (z_at * 2 + lax.rem(x_at, 2)) * 4 + y_at,
            lax.div(x_at, 2) * 2 + core_at,
        )

    def zo(o):
        return lax.rem(z + o + 8, 8)

    def xo(o):
        return lax.rem(x + o + 4, 4)

    def yo(o):
        return lax.rem(y + o + 4, 4)

    def to_z(o):
        return at(z_at=zo(o))

    def to_x(o):
        return at(x_at=xo(o))

    def to_y(o):
        return at(y_at=yo(o))

    across = at(x_at=xh * 2 + 1 - xl)
    twin = at(core_at=1 - core)

    started = []

    def message(src, dst, where):
        k = len(started)
        copy = pltpu.make_async_remote_copy(
            src_ref=src, dst_ref=dst, send_sem=s.send_sem.at[k], recv_sem=s.recv_sem.at[k],
            device_id=where, device_id_type=MESH,
        )
        copy.start()
        started.append(copy)
        return copy

    flushed = [0]

    def flush(upto):
        for copy in started[flushed[0] : upto]:
            copy.wait_send()
        flushed[0] = max(upto, flushed[0])

    def lanes(half):
        return pl.ds(pl.multiple_of(half * W, 128), W)

    def rows(span):
        return pl.ds(span[0], span[1])

    def length_of(n, q, way):
        return n // 2 - (q + way) % 2

    def gather(view, to, n):
        flows = {}

        def start(q):
            for way, sign in ((0, 1), (1, -1)):
                flows[way, q, 1] = message(view(0, q), view(0, q), to(sign))

        def advance(step, q):
            for way, sign in ((0, 1), (1, -1)):
                length = length_of(n, q, way)
                if step <= length:
                    flows[way, q, step].wait_recv()
                if step < length:
                    block = view(-sign * step, q)
                    flows[way, q, step + 1] = message(block, block, to(sign))

        return start, advance

    def reduce(name, piece, to, n, finish, count, last_to=None):
        flows = {}

        def buffer(kind, q, way, step):
            return getattr(s, f"{name}_{kind}{q}").at[way, step - 1]

        for step in range(1, n // 2 + 1):
            for q in range(count):
                for way, sign in ((0, 1), (1, -1)):
                    first = n // 2 + 1 - length_of(n, q, way)
                    if step < first:
                        continue
                    value = piece(q, sign * (n // 2 + 1 - step))
                    if step > first:
                        flows[way, q, step - 1].wait_recv()
                        value = value + buffer("r", q, way, step - 1)[...].astype(F32)
                    buffer("s", q, way, step)[...] = value.astype(BF16)
                    where = to(sign) if step < n // 2 or last_to is None else last_to(q, sign)
                    flows[way, q, step] = message(buffer("s", q, way, step), buffer("r", q, way, step), where)
            yield
        for q in range(count):
            total = None
            for way in (0, 1):
                flows[way, q, n // 2].wait_recv()
                value = buffer("r", q, way, n // 2)[...].astype(F32)
                total = value if total is None else total + value
            finish(q, total)
        yield

    barrier = pltpu.get_barrier_semaphore()
    peers = [at(x_at=xo(a), y_at=yo(b)) for a in range(4) for b in range(4) if a or b]
    peers += [to_z(o) for o in range(1, 8)]
    peers += [twin, at(x_at=xo(2), core_at=1 - core)] + [at(z_at=zo(o), x_at=xo(2)) for o in (1, -1)]
    loads = [
        pltpu.make_async_copy(src, dst, s.load_sem.at[k])
        for k, (src, dst) in enumerate((
            (th_any, s.th), (tf_any, s.tf), (xh_any, s.xh), (xf_any, s.xf), (log_temp, s.scale), (logit_bias, s.bias)
        ))
    ]
    for copy in loads:
        copy.start()
    for peer in peers:
        pl.semaphore_signal(barrier, inc=1, device_id=peer, device_id_type=MESH)

    def padded(value, count):
        return jnp.concatenate([value, jnp.zeros((count - value.shape[0],) + value.shape[1:], value.dtype)], axis=0)

    def send_sums(ref, value):
        wide = jnp.broadcast_to(jnp.sum(value, axis=1, keepdims=True), (RT, 128))
        ref[mp] = padded(wide, 256).T[0:8]

        def send():
            return [
                message(ref.at[mp], ref.at[mp], where)
                for where in (twin, to_x(2), at(x_at=xo(2), core_at=1 - core))
            ]

        return send

    def sums_of(ref, got):
        for copy in got:
            copy.wait_recv()
        return (ref[0] + ref[1]) + (ref[2] + ref[3])

    def down(total):
        return jnp.broadcast_to(total[0:1], (128, 256)).T[0:RT]

    def over_xy(src, dst, place=None):
        copies = []
        for a in (1, 0):
            for b in (2, 1, 3, 0):
                if a or b:
                    to_xl = lax.rem(xl + a, 2)
                    where = at(x_at=xh * 2 + to_xl, y_at=yo(b))
                    if place is None:
                        copies.append(message(src.at[to_xl * 4 + yo(b)], dst.at[a * 4 + b - 1], where))
                    else:
                        copies.append(message(src.at[place], dst.at[place], where))
        return copies

    loads[0].wait()
    loads[1].wait()
    txt_pre = padded(jnp.dot(s.tf[...], s.th[...], preferred_element_type=F32), RT)
    s.dir_t[...] = txt_pre
    send_t = send_sums(s.sums_t, txt_pre * txt_pre)
    own = lanes(xh)
    kinds = (own, lanes(1 - xh))
    s.texts_a[xl, y, :, own] = txt_pre[0:RA].astype(BF16)
    s.texts_b[xl, y, :, own] = txt_pre[RA:RT].astype(BF16)
    pl.semaphore_wait(barrier, len(peers))

    sent_t = send_t()
    view = s.texts_a.at[xl, y, :, own]
    go_a1 = [message(view, view, to_x(o)) for o in (1, 2, 3)]
    view = s.texts_b.at[xl, y, :, own]
    go_b1 = [message(view, view, to_y(o)) for o in (1, 2, 3)]
    loads[2].wait()
    loads[3].wait()
    img_pre = padded(jnp.dot(s.xf[...], s.xh[...], preferred_element_type=F32), RT)
    s.dir_i[...] = img_pre
    s.parts[0] = padded(img_pre[0:64], RI).astype(BF16)
    s.parts[1] = img_pre[64:144].astype(BF16)
    swap = message(s.parts.at[1 - xh], s.images.at[z, :, own], to_x(2))
    s.images[z, :, own] = s.parts[xh]

    def image_chunk(o, q):
        kind, span = I_CHUNKS[q]
        return s.images.at[zo(o), rows(span), kinds[kind]]

    start, advance = gather(image_chunk, to_z, 8)
    start(0)
    start(1)
    sent_i = send_sums(s.sums_i, img_pre * img_pre)()
    s.all_t[slot] = sums_of(s.sums_t, sent_t)
    norms_t = over_xy(s.all_t, s.all_t, slot)
    swap.wait_recv()
    start(2)
    start(3)
    advance(1, 0)
    advance(1, 1)
    for copy in go_a1:
        copy.wait_recv()
    view = s.texts_a.at[:, y]
    go_a2 = [message(view, view, to_y(o)) for o in (1, 2, 3)]
    for copy in go_b1:
        copy.wait_recv()
    view = s.texts_b.at[xl, :, :, own]
    go_b2 = [message(view, view, to_x(o)) for o in (1, 2, 3)]
    s.all_i[z] = sums_of(s.sums_i, sent_i)
    norms_i = [message(s.all_i.at[z], s.all_i.at[z], to_z(o)) for o in range(1, 8)]
    advance(1, 2)
    advance(1, 3)
    for name, place in (("t", slot), ("i", z)):
        norm = jnp.sqrt(down(getattr(s, f"all_{name}")[place]) + 1e-06)
        getattr(s, f"norm_{name}")[...] = norm
        side = getattr(s, f"dir_{name}")
        side[...] = side[...] / norm[:, 0:1]
    for q in range(4):
        advance(2, q)

    def columns_of(name, copies):
        for copy in copies:
            copy.wait_recv()
        every = getattr(s, f"all_{name}")
        sums = jnp.concatenate([every[k if name == "t" else zo(k), 0:1] for k in range(8)], axis=0)
        getattr(s, f"columns_{name}")[...] = padded(1.0 / jnp.sqrt(sums + 1e-06), 128).T

    def image_units(*distances):
        for o in distances:
            scale = s.columns_i[pl.ds(pl.multiple_of(xh * 64, 8), RI), o % 8 : o % 8 + 1]
            s.images_n[zo(o)] = (s.images[zo(o)].astype(F32) * scale).astype(BF16)

    columns_of("t", norms_t)
    columns_of("i", norms_i)
    image_units(0, 1, -1)
    for q in range(4):
        advance(3, q)
    image_units(2, -2, 3, -3)
    for q in range(4):
        advance(4, q)
    image_units(4)

    def text_units(part, first, count, copies):
        for copy in copies:
            copy.wait_recv()
        texts, units = getattr(s, f"texts_{part}"), getattr(s, f"texts_{part}n")
        for k in range(8):
            units[k // 4, k % 4] = (
                texts[k // 4, k % 4].astype(F32) * s.columns_t[pl.ds(first, count), k : k + 1]
            ).astype(BF16)

    loads[4].wait()
    loads[5].wait()
    temper = jnp.exp(jnp.full((1, 128), s.scale[0], F32))[:, 0:1]
    bias = s.bias[0]
    half = pl.ds(core * 4, 4)

    def products(part, count):
        texts, theirs, got, mine = (
            getattr(s, k) for k in (f"texts_{part}n", f"theirs_{part}", f"got_{part}", f"mine_{part}")
        )
        columns = texts[...].reshape(8 * count, 2 * W)
        theirs[...] = lax.dot_general(
            s.images_n[pl.ds((1 - core) * 4, 4)].reshape(4 * RI, 2 * W), columns, NT, preferred_element_type=F32
        ).reshape(4, RI, 8 * count)
        cross = message(theirs, got, twin)
        mine[...] = lax.dot_general(
            s.images_n[half].reshape(4 * RI, 2 * W), columns, NT, preferred_element_type=F32
        ).reshape(4, RI, 8 * count)
        return cross

    def pairs(part, count, first, cross):
        got, mine, pg = (getattr(s, f"{k}_{part}") for k in ("got", "mine", "pg"))
        shape = (RI, 8 * count)
        ahead = lax.broadcasted_iota(jnp.int32, shape, 1) - lax.broadcasted_iota(jnp.int32, shape, 0)
        column = lax.broadcasted_iota(jnp.int32, (1, 8 * count), 1) - slot * count
        here = (column >= 0) & (column < count)
        cross.wait_recv()

        @pl.loop(0, 4)
        def _(block):
            logits = temper * (mine[block] + got[block]) + bias
            same = here & (ahead == jnp.where(core * 4 + block == z, slot * count + 64 * xh - first, -8192))
            pg[core * 4 + block] = (temper * (jax.nn.sigmoid(logits) - same.astype(F32))).astype(BF16)

        return message(pg.at[half], pg.at[half], twin)

    def text_grads(part, count):
        pg, grad, grad_s = (getattr(s, k) for k in (f"pg_{part}", f"grad_{part}", f"grad_{part}s"))
        value = lax.dot_general(
            pg[...].reshape(8 * RI, 8 * count), s.images_n[...].reshape(8 * RI, 2 * W), TN, preferred_element_type=F32
        ).reshape(2, 4, count, 2 * W)
        grad[...] = value
        grad_s[...] = value.astype(BF16)

    text_units("a", 0, RA, go_a2)
    cross_a = products("a", RA)
    share_a = pairs("a", RA, 0, cross_a)
    text_units("b", RA, RB, go_b2)
    arrived = len(started)
    cross_b = products("b", RB)
    share_a.wait_recv()
    text_grads("a", RA)
    back_a1 = [message(s.grad_as.at[:, yo(o)], s.a1.at[o - 1], to_y(o)) for o in (1, 2, 3)]
    share_b = pairs("b", RB, RA, cross_b)
    s.grad_i[...] = lax.dot_general(
        s.pg_a[...].reshape(8 * RI, 8 * RA), s.texts_an[...].reshape(8 * RA, 2 * W), NN, preferred_element_type=F32
    ).reshape(8, RI, 2 * W)
    share_b.wait_recv()
    text_grads("b", RB)
    back_b1 = [
        message(s.grad_bs.at[lax.rem(xo(o), 2), :, :, lanes(lax.div(xo(o), 2))], s.b1.at[o - 1], to_x(o))
        for o in (1, 2, 3)
    ]
    s.grad_i[...] += lax.dot_general(
        s.pg_b[...].reshape(8 * RI, 8 * RB), s.texts_bn[...].reshape(8 * RB, 2 * W), NN, preferred_element_type=F32
    ).reshape(8, RI, 2 * W)

    def image_term(q, o):
        kind, span = I_CHUNKS[q]
        return s.grad_i[zo(o), rows(span), kinds[kind]]

    def image_done(q, total):
        kind, span = I_CHUNKS[q]
        if kind == 0:
            s.both[xh, rows(span)] = total + image_term(q, 0)
        else:
            s.both[1 - xh, rows(span)] = total

    back_z = reduce(
        "img", image_term, to_z, 8, image_done, 4,
        lambda q, sign: to_z(sign) if I_CHUNKS[q][0] == 0 else at(z_at=zo(sign), x_at=xo(2)),
    )
    next(back_z)
    s.swap_s[...] = s.grad_i[z, :, kinds[1]].astype(BF16)
    swap_back = message(s.swap_s, s.swap_r, to_x(2))
    flush(arrived)
    next(back_z)
    next(back_z)
    for copy in back_a1:
        copy.wait_recv()
    s.a_sum[...] = s.grad_a[:, y] + sum(s.a1[o].astype(F32) for o in range(3))
    s.a_s[...] = s.a_sum[...].astype(BF16)
    back_a2 = [
        message(s.a_s.at[lax.rem(xo(o), 2), :, lanes(lax.div(xo(o), 2))], s.a2.at[o - 1], to_x(o)) for o in (1, 2, 3)
    ]
    next(back_z)
    for copy in back_b1:
        copy.wait_recv()
    s.b_sum[...] = s.grad_b[xl, :, :, own] + sum(s.b1[o].astype(F32) for o in range(3))
    s.b_s[...] = s.b_sum[...].astype(BF16)
    back_b2 = [message(s.b_s.at[yo(o)], s.b2.at[o - 1], to_y(o)) for o in (1, 2, 3)]
    next(back_z)
    swap_back.wait_recv()
    s.both[1 - xh] += s.swap_r[...].astype(F32)
    img_unit_grad = jnp.concatenate([s.both[0, pl.ds(0, 64)], s.both[1]], axis=0)
    returned = len(started)
    sent_i = send_sums(s.along_i, img_unit_grad * s.dir_i[...])()
    for copy in back_a2:
        copy.wait_recv()
    s.t_sum[pl.ds(0, RA)] = s.a_sum[xl, :, own] + sum(s.a2[o].astype(F32) for o in range(3))
    for copy in back_b2:
        copy.wait_recv()
    s.t_sum[pl.ds(RA, RB)] = s.b_sum[y] + sum(s.b2[o].astype(F32) for o in range(3))
    sent_t = send_sums(s.along_t, s.t_sum[...] * s.dir_t[...])()

    along = down(sums_of(s.along_i, sent_i))
    img_unit_grad = jnp.concatenate([s.both[0, pl.ds(0, 64)], s.both[1]], axis=0)
    img_grad = ((img_unit_grad - s.dir_i[...] * along[:, 0:1]) / s.norm_i[:, 0:1]).astype(BF16)
    s.head_i[...] = lax.dot_general(s.xf[...], img_grad[0:R], TN, preferred_element_type=F32)
    sides = ((pl.ds(0, 256), s.si0, s.ri0, s.zi_s0, s.zi_r0), (pl.ds(256, 128), s.si1, s.ri1, s.zi_s1, s.zi_r1))
    for span, si, _, _, _ in sides:
        for j in range(8):
            si[j] = jnp.concatenate([s.head_i[pl.ds(k * 192 + j * 24, 24), span] for k in range(8)], axis=0).astype(BF16)

    fore_i = [over_xy(si, ri) for _, si, ri, _, _ in sides]
    along = down(sums_of(s.along_t, sent_t))
    txt_grad = ((s.t_sum[...] - s.dir_t[...] * along[:, 0:1]) / s.norm_t[:, 0:1]).astype(BF16)
    s.head_t[...] = lax.dot_general(s.tf[...], txt_grad[0:R], TN, preferred_element_type=F32)

    def text_term(q, o):
        return s.head_t[pl.ds(pl.multiple_of(zo(o) * RT + T_CHUNKS[q][0], 16), T_CHUNKS[q][1]), :]

    def text_done(q, total):
        s.t_sum[rows(T_CHUNKS[q])] = total + text_term(q, 0)

    fore_t = reduce("ht", text_term, to_z, 8, text_done, 4)
    next(fore_t)
    flush(returned)
    next(fore_t)
    next(fore_t)
    next(fore_t)
    last_i = []
    for side, (span, _, ri, zi_s, zi_r) in enumerate(sides):
        if side == 1:
            next(fore_t)
            before = len(started)
            total = s.t_sum[...]
            for j in range(8):
                s.xt[j] = padded(total[18 * j : 18 * j + 18], 24)
            last_t = over_xy(s.xt, s.xt_r)
        for copy in fore_i[side]:
            copy.wait_recv()
        whole = sum(ri[j].astype(F32) for j in range(7))
        for k in range(8):
            s.zi[k, :, span] = (
                s.head_i[pl.ds(pl.multiple_of(k * 192 + slot * 24, 8), 24), span] + whole[k * 24 : k * 24 + 24]
            )
            zi_s[k] = padded(s.zi[k, :, span], 32).astype(BF16)
        last_i.append([message(zi_s.at[zo(o)], zi_r.at[o - 1], to_z(o)) for o in (4, 3, 5, 2, 6, 1, 7)])
    flush(before)
    for copy in last_t:
        copy.wait_recv()
    out_t[...] = (s.xt[slot] + sum(s.xt_r[j] for j in range(7)))[0:18]
    for (span, _, _, _, zi_r), copies in zip(sides, last_i):
        for copy in copies:
            copy.wait_recv()
        out_i[:, span] = s.zi[z, :, span] + sum(zi_r[j].astype(F32) for j in range(7))[0:24]
    flush(len(started))


def body(image_feats, text_feats, image_head, text_head, log_temp, logit_bias):
    vmem = pl.BlockSpec(memory_space=pltpu.VMEM)
    anywhere = pl.BlockSpec(memory_space=pl.ANY)
    scratch = scratch_of()

    def run(*refs):
        kernel(tuple(scratch), *refs)

    found = pl.pallas_call(
        run,
        out_shape=(jax.ShapeDtypeStruct((24, W), F32), jax.ShapeDtypeStruct((18, W), F32)),
        in_specs=[anywhere] * 6,
        out_specs=(vmem, vmem),
        scratch_shapes=list(scratch.values()),
        compiler_params=pltpu.CompilerParams(
            collective_id=0, has_side_effects=True, vmem_limit_bytes=56 * 1024 * 1024
        ),
        name="pair_loss",
    )(image_feats, text_feats, image_head, text_head, log_temp, logit_bias)

    def hand_over(a, b, c, d):
        c[...] = a[...]
        d[...] = b[...]

    return pl.pallas_call(
        hand_over,
        out_shape=(jax.ShapeDtypeStruct((24, W), F32), jax.ShapeDtypeStruct((18, W), F32)),
        in_specs=[vmem, vmem],
        out_specs=(vmem, vmem),
        name="hand_over",
    )(*found)


def solution(mesh):
    placed = (P("dp", None), P("dp", None), P(None, "mp"), P(None, "mp"), P(), P())
    return jax.shard_map(
        body, mesh=mesh, in_specs=placed, out_specs=(P("dp", "mp"), P("dp", "mp")), check_vma=False
    )
```

```python
import types

import jax
import jax.numpy as jnp
from jax import lax
from jax.experimental import pallas as pl
from jax.experimental.pallas import tpu as pltpu
from jax.sharding import PartitionSpec as P

F32 = jnp.float32
BF16 = jnp.bfloat16
MESH = pl.DeviceIdType.MESH
NT = (((1,), (1,)), ((), ()))
TN = (((0,), (0,)), ((), ()))
NN = (((1,), (0,)), ((), ()))
R = 136
RT = 144
RI = 80
W = 384
MESSAGES = 200
RA, RB = 80, 64
I_CHUNKS = ((0, (0, 48)), (0, (48, 32)), (1, (0, 48)), (1, (48, 32)))
T_CHUNKS = ((0, 32), (32, 32), (64, 32), (96, 48))


def f32(*shape):
    return pltpu.VMEM(shape, F32)


def bf16(*shape):
    return pltpu.VMEM(shape, BF16)


def scratch_of():
    made = dict(
        xf=bf16(R, 1536), tf=bf16(R, 1152), xh=bf16(1536, W), th=bf16(1152, W),
        sums_t=f32(4, 8, 256), sums_i=f32(4, 8, 256), along_t=f32(4, 8, 256), along_i=f32(4, 8, 256),
        norm_t=f32(RT, 128), norm_i=f32(RT, 128), dir_t=f32(RT, W), dir_i=f32(RT, W),
        parts=bf16(2, RI, W), texts_a=bf16(2, 4, RA, 2 * W), texts_b=bf16(2, 4, RB, 2 * W), images=bf16(8, RI, 2 * W),
        mine_a=f32(4, RI, 8 * RA), theirs_a=f32(4, RI, 8 * RA), got_a=f32(4, RI, 8 * RA), pg_a=bf16(8, RI, 8 * RA),
        mine_b=f32(4, RI, 8 * RB), theirs_b=f32(4, RI, 8 * RB), got_b=f32(4, RI, 8 * RB), pg_b=bf16(8, RI, 8 * RB),
        grad_i=f32(8, RI, 2 * W), grad_a=f32(2, 4, RA, 2 * W), grad_b=f32(2, 4, RB, 2 * W),
        grad_as=bf16(2, 4, RA, 2 * W), grad_bs=bf16(2, 4, RB, 2 * W),
        a1=bf16(3, 2, RA, 2 * W), a_sum=f32(2, RA, 2 * W), a_s=bf16(2, RA, 2 * W), a2=bf16(3, RA, W),
        b1=bf16(3, 4, RB, W), b_sum=f32(4, RB, W), b_s=bf16(4, RB, W), b2=bf16(3, RB, W),
        swap_s=bf16(RI, W), swap_r=bf16(RI, W), both=f32(2, RI, W), t_sum=f32(RT, W),
        head_t=f32(1152, W), head_i=f32(1536, W), si0=bf16(8, 192, 256), ri0=bf16(7, 192, 256), si1=bf16(8, 192, 128), ri1=bf16(7, 192, 128),
        zi=f32(8, 24, W), zi_s0=bf16(8, 32, 256), zi_r0=bf16(7, 32, 256), zi_s1=bf16(8, 32, 128), zi_r1=bf16(7, 32, 128), xt=f32(8, 24, W), xt_r=f32(7, 24, W),
    )

    def ring(name, steps, *shapes):
        for q, shape in enumerate(shapes):
            made[f"{name}_s{q}"] = bf16(2, steps, *shape)
            made[f"{name}_r{q}"] = bf16(2, steps, *shape)

    ring("img", 4, *((n, W) for _, (_, n) in I_CHUNKS))
    ring("ht", 4, *((n, W) for _, n in T_CHUNKS))
    made.update(
        send_sem=pltpu.SemaphoreType.DMA((MESSAGES,)),
        recv_sem=pltpu.SemaphoreType.DMA((MESSAGES,)),
        load_sem=pltpu.SemaphoreType.DMA((4,)),
    )
    return made


def kernel(names, xf_any, tf_any, xh_any, th_any, log_temp, logit_bias, out_i, out_t, *refs):
    s = types.SimpleNamespace(**dict(zip(names, refs)))
    dp, mp = lax.axis_index("dp"), lax.axis_index("mp")
    z, xl, y = lax.div(dp, 8), lax.rem(lax.div(dp, 4), 2), lax.rem(dp, 4)
    xh, core = lax.div(mp, 2), lax.rem(mp, 2)
    x = xh * 2 + xl
    slot = xl * 4 + y

    def at(z_at=None, x_at=None, y_at=None, core_at=None):
        z_at = z if z_at is None else z_at
        x_at = x if x_at is None else x_at
        y_at = y if y_at is None else y_at
        core_at = core if core_at is None else core_at
        return (
            (z_at * 2 + lax.rem(x_at, 2)) * 4 + y_at,
            lax.div(x_at, 2) * 2 + core_at,
        )

    def zo(o):
        return lax.rem(z + o + 8, 8)

    def xo(o):
        return lax.rem(x + o + 4, 4)

    def yo(o):
        return lax.rem(y + o + 4, 4)

    def to_z(o):
        return at(z_at=zo(o))

    def to_x(o):
        return at(x_at=xo(o))

    def to_y(o):
        return at(y_at=yo(o))

    across = at(x_at=xh * 2 + 1 - xl)
    twin = at(core_at=1 - core)

    started = []

    def message(src, dst, where):
        k = len(started)
        copy = pltpu.make_async_remote_copy(
            src_ref=src, dst_ref=dst, send_sem=s.send_sem.at[k], recv_sem=s.recv_sem.at[k],
            device_id=where, device_id_type=MESH,
        )
        copy.start()
        started.append(copy)
        return copy

    flushed = [0]

    def flush(upto):
        for copy in started[flushed[0] : upto]:
            copy.wait_send()
        flushed[0] = max(upto, flushed[0])

    def lanes(half):
        return pl.ds(pl.multiple_of(half * W, 128), W)

    def rows(span):
        return pl.ds(span[0], span[1])

    def length_of(n, q, way):
        return n // 2 - (q + way) % 2

    def gather(view, to, n):
        flows = {}

        def start(q):
            for way, sign in ((0, 1), (1, -1)):
                flows[way, q, 1] = message(view(0, q), view(0, q), to(sign))

        def advance(step, q):
            for way, sign in ((0, 1), (1, -1)):
                length = length_of(n, q, way)
                if step <= length:
                    flows[way, q, step].wait_recv()
                if step < length:
                    block = view(-sign * step, q)
                    flows[way, q, step + 1] = message(block, block, to(sign))

        return start, advance

    def reduce(name, piece, to, n, finish, count, last_to=None):
        flows = {}

        def buffer(kind, q, way, step):
            return getattr(s, f"{name}_{kind}{q}").at[way, step - 1]

        for step in range(1, n // 2 + 1):
            for q in range(count):
                for way, sign in ((0, 1), (1, -1)):
                    first = n // 2 + 1 - length_of(n, q, way)
                    if step < first:
                        continue
                    value = piece(q, sign * (n // 2 + 1 - step))
                    if step > first:
                        flows[way, q, step - 1].wait_recv()
                        value = value + buffer("r", q, way, step - 1)[...].astype(F32)
                    buffer("s", q, way, step)[...] = value.astype(BF16)
                    where = to(sign) if step < n // 2 or last_to is None else last_to(q, sign)
                    flows[way, q, step] = message(buffer("s", q, way, step), buffer("r", q, way, step), where)
            yield
        for q in range(count):
            total = None
            for way in (0, 1):
                flows[way, q, n // 2].wait_recv()
                value = buffer("r", q, way, n // 2)[...].astype(F32)
                total = value if total is None else total + value
            finish(q, total)
        yield

    barrier = pltpu.get_barrier_semaphore()
    peers = [at(x_at=xo(a), y_at=yo(b)) for a in range(4) for b in range(4) if a or b]
    peers += [to_z(o) for o in range(1, 8)]
    peers += [twin, at(x_at=xo(2), core_at=1 - core)] + [at(z_at=zo(o), x_at=xo(2)) for o in (1, -1)]
    loads = [
        pltpu.make_async_copy(src, dst, s.load_sem.at[k])
        for k, (src, dst) in enumerate(((th_any, s.th), (tf_any, s.tf), (xh_any, s.xh), (xf_any, s.xf)))
    ]
    for copy in loads:
        copy.start()
    for peer in peers:
        pl.semaphore_signal(barrier, inc=1, device_id=peer, device_id_type=MESH)

    def padded(value, count):
        return jnp.concatenate([value, jnp.zeros((count - value.shape[0],) + value.shape[1:], value.dtype)], axis=0)

    def send_sums(ref, value):
        wide = jnp.broadcast_to(jnp.sum(value, axis=1, keepdims=True), (RT, 128))
        ref[mp] = padded(wide, 256).T[0:8]

        def send():
            return [
                message(ref.at[mp], ref.at[mp], where)
                for where in (twin, to_x(2), at(x_at=xo(2), core_at=1 - core))
            ]

        return send

    def sums_of(ref, got):
        for copy in got:
            copy.wait_recv()
        total = (ref[0] + ref[1]) + (ref[2] + ref[3])
        return jnp.broadcast_to(total[0:1], (128, 256)).T[0:RT]

    loads[0].wait()
    loads[1].wait()
    txt_pre = padded(jnp.dot(s.tf[...], s.th[...], preferred_element_type=F32), RT)
    s.dir_t[...] = txt_pre
    send_t = send_sums(s.sums_t, txt_pre * txt_pre)
    pl.semaphore_wait(barrier, len(peers))
    sent_t = send_t()
    loads[2].wait()
    loads[3].wait()
    img_pre = padded(jnp.dot(s.xf[...], s.xh[...], preferred_element_type=F32), RT)
    s.dir_i[...] = img_pre
    sent_i = send_sums(s.sums_i, img_pre * img_pre)()
    norm = jnp.sqrt(sums_of(s.sums_t, sent_t) + 1e-06)
    s.norm_t[...] = norm
    txt_dir = s.dir_t[...] / norm[:, 0:1]
    s.dir_t[...] = txt_dir

    own = lanes(xh)
    kinds = (own, lanes(1 - xh))
    s.texts_a[xl, y, :, own] = txt_dir[0:RA].astype(BF16)
    s.texts_b[xl, y, :, own] = txt_dir[RA:RT].astype(BF16)
    view = s.texts_a.at[xl, y, :, own]
    go_a1 = [message(view, view, to_x(o)) for o in (1, 2, 3)]
    view = s.texts_b.at[xl, y, :, own]
    go_b1 = [message(view, view, to_y(o)) for o in (1, 2, 3)]
    norm = jnp.sqrt(sums_of(s.sums_i, sent_i) + 1e-06)
    s.norm_i[...] = norm
    img_dir = s.dir_i[...] / norm[:, 0:1]
    s.dir_i[...] = img_dir
    s.parts[0] = padded(img_dir[0:64], RI).astype(BF16)
    s.parts[1] = img_dir[64:144].astype(BF16)
    swap = message(s.parts.at[1 - xh], s.images.at[z, :, own], to_x(2))
    s.images[z, :, own] = s.parts[xh]

    def image_chunk(o, q):
        kind, span = I_CHUNKS[q]
        return s.images.at[zo(o), rows(span), kinds[kind]]

    start, advance = gather(image_chunk, to_z, 8)
    start(0)
    start(1)
    swap.wait_recv()
    start(2)
    start(3)
    advance(1, 0)
    advance(1, 1)
    for copy in go_a1:
        copy.wait_recv()
    view = s.texts_a.at[:, y]
    go_a2 = [message(view, view, to_y(o)) for o in (1, 2, 3)]
    for copy in go_b1:
        copy.wait_recv()
    view = s.texts_b.at[xl, :, :, own]
    go_b2 = [message(view, view, to_x(o)) for o in (1, 2, 3)]
    advance(1, 2)
    advance(1, 3)
    for step in (2, 3, 4):
        for q in range(4):
            advance(step, q)

    temper = jnp.exp(jnp.full((1, 128), log_temp[0], F32))[:, 0:1]
    bias = logit_bias[0]
    half = pl.ds(core * 4, 4)

    def products(part, count):
        texts, theirs, got, mine = (getattr(s, f"{k}_{part}") for k in ("texts", "theirs", "got", "mine"))
        columns = texts[...].reshape(8 * count, 2 * W)
        theirs[...] = lax.dot_general(
            s.images[pl.ds((1 - core) * 4, 4)].reshape(4 * RI, 2 * W), columns, NT, preferred_element_type=F32
        ).reshape(4, RI, 8 * count)
        cross = message(theirs, got, twin)
        mine[...] = lax.dot_general(
            s.images[half].reshape(4 * RI, 2 * W), columns, NT, preferred_element_type=F32
        ).reshape(4, RI, 8 * count)
        return cross

    def pairs(part, count, first, cross):
        got, mine, pg = (getattr(s, f"{k}_{part}") for k in ("got", "mine", "pg"))
        shape = (RI, 8 * count)
        ahead = lax.broadcasted_iota(jnp.int32, shape, 1) - lax.broadcasted_iota(jnp.int32, shape, 0)
        column = lax.broadcasted_iota(jnp.int32, (1, 8 * count), 1) - slot * count
        here = (column >= 0) & (column < count)
        cross.wait_recv()

        @pl.loop(0, 4)
        def _(block):
            logits = temper * (mine[block] + got[block]) + bias
            same = here & (ahead == jnp.where(core * 4 + block == z, slot * count + 64 * xh - first, -8192))
            pg[core * 4 + block] = (temper * (jax.nn.sigmoid(logits) - same.astype(F32))).astype(BF16)

        return message(pg.at[half], pg.at[half], twin)

    def text_grads(part, count):
        pg, grad, grad_s = (getattr(s, k) for k in (f"pg_{part}", f"grad_{part}", f"grad_{part}s"))
        value = lax.dot_general(
            pg[...].reshape(8 * RI, 8 * count), s.images[...].reshape(8 * RI, 2 * W), TN, preferred_element_type=F32
        ).reshape(2, 4, count, 2 * W)
        grad[...] = value
        grad_s[...] = value.astype(BF16)

    for copy in go_a2:
        copy.wait_recv()
    cross_a = products("a", RA)
    share_a = pairs("a", RA, 0, cross_a)
    for copy in go_b2:
        copy.wait_recv()
    arrived = len(started)
    cross_b = products("b", RB)
    share_a.wait_recv()
    text_grads("a", RA)
    back_a1 = [message(s.grad_as.at[:, yo(o)], s.a1.at[o - 1], to_y(o)) for o in (1, 2, 3)]
    share_b = pairs("b", RB, RA, cross_b)
    s.grad_i[...] = lax.dot_general(
        s.pg_a[...].reshape(8 * RI, 8 * RA), s.texts_a[...].reshape(8 * RA, 2 * W), NN, preferred_element_type=F32
    ).reshape(8, RI, 2 * W)
    share_b.wait_recv()
    text_grads("b", RB)
    back_b1 = [
        message(s.grad_bs.at[lax.rem(xo(o), 2), :, :, lanes(lax.div(xo(o), 2))], s.b1.at[o - 1], to_x(o))
        for o in (1, 2, 3)
    ]
    s.grad_i[...] += lax.dot_general(
        s.pg_b[...].reshape(8 * RI, 8 * RB), s.texts_b[...].reshape(8 * RB, 2 * W), NN, preferred_element_type=F32
    ).reshape(8, RI, 2 * W)

    def image_term(q, o):
        kind, span = I_CHUNKS[q]
        return s.grad_i[zo(o), rows(span), kinds[kind]]

    def image_done(q, total):
        kind, span = I_CHUNKS[q]
        if kind == 0:
            s.both[xh, rows(span)] = total + image_term(q, 0)
        else:
            s.both[1 - xh, rows(span)] = total

    back_z = reduce(
        "img", image_term, to_z, 8, image_done, 4,
        lambda q, sign: to_z(sign) if I_CHUNKS[q][0] == 0 else at(z_at=zo(sign), x_at=xo(2)),
    )
    next(back_z)
    s.swap_s[...] = s.grad_i[z, :, kinds[1]].astype(BF16)
    swap_back = message(s.swap_s, s.swap_r, to_x(2))
    flush(arrived)
    next(back_z)
    next(back_z)
    for copy in back_a1:
        copy.wait_recv()
    s.a_sum[...] = s.grad_a[:, y] + sum(s.a1[o].astype(F32) for o in range(3))
    s.a_s[...] = s.a_sum[...].astype(BF16)
    back_a2 = [
        message(s.a_s.at[lax.rem(xo(o), 2), :, lanes(lax.div(xo(o), 2))], s.a2.at[o - 1], to_x(o)) for o in (1, 2, 3)
    ]
    for copy in back_b1:
        copy.wait_recv()
    s.b_sum[...] = s.grad_b[xl, :, :, own] + sum(s.b1[o].astype(F32) for o in range(3))
    s.b_s[...] = s.b_sum[...].astype(BF16)
    back_b2 = [message(s.b_s.at[yo(o)], s.b2.at[o - 1], to_y(o)) for o in (1, 2, 3)]
    next(back_z)
    next(back_z)
    swap_back.wait_recv()
    s.both[1 - xh] += s.swap_r[...].astype(F32)
    img_unit_grad = jnp.concatenate([s.both[0, pl.ds(0, 64)], s.both[1]], axis=0)
    returned = len(started)
    sent_i = send_sums(s.along_i, img_unit_grad * s.dir_i[...])()
    for copy in back_a2:
        copy.wait_recv()
    s.t_sum[pl.ds(0, RA)] = s.a_sum[xl, :, own] + sum(s.a2[o].astype(F32) for o in range(3))
    for copy in back_b2:
        copy.wait_recv()
    s.t_sum[pl.ds(RA, RB)] = s.b_sum[y] + sum(s.b2[o].astype(F32) for o in range(3))
    sent_t = send_sums(s.along_t, s.t_sum[...] * s.dir_t[...])()

    along = sums_of(s.along_i, sent_i)
    img_unit_grad = jnp.concatenate([s.both[0, pl.ds(0, 64)], s.both[1]], axis=0)
    img_grad = ((img_unit_grad - s.dir_i[...] * along[:, 0:1]) / s.norm_i[:, 0:1]).astype(BF16)
    s.head_i[...] = lax.dot_general(s.xf[...], img_grad[0:R], TN, preferred_element_type=F32)
    sides = ((pl.ds(0, 256), s.si0, s.ri0, s.zi_s0, s.zi_r0), (pl.ds(256, 128), s.si1, s.ri1, s.zi_s1, s.zi_r1))
    for span, si, _, _, _ in sides:
        for j in range(8):
            si[j] = jnp.concatenate([s.head_i[pl.ds(k * 192 + j * 24, 24), span] for k in range(8)], axis=0).astype(BF16)

    def over_xy(src, dst):
        copies = []
        for a in (1, 0):
            for b in (2, 1, 3, 0):
                if a or b:
                    to_xl = lax.rem(xl + a, 2)
                    where = at(x_at=xh * 2 + to_xl, y_at=yo(b))
                    copies.append(message(src.at[to_xl * 4 + yo(b)], dst.at[a * 4 + b - 1], where))
        return copies

    fore_i = [over_xy(si, ri) for _, si, ri, _, _ in sides]
    along = sums_of(s.along_t, sent_t)
    txt_grad = ((s.t_sum[...] - s.dir_t[...] * along[:, 0:1]) / s.norm_t[:, 0:1]).astype(BF16)
    s.head_t[...] = lax.dot_general(s.tf[...], txt_grad[0:R], TN, preferred_element_type=F32)

    def text_term(q, o):
        return s.head_t[pl.ds(pl.multiple_of(zo(o) * RT + T_CHUNKS[q][0], 16), T_CHUNKS[q][1]), :]

    def text_done(q, total):
        s.t_sum[rows(T_CHUNKS[q])] = total + text_term(q, 0)

    fore_t = reduce("ht", text_term, to_z, 8, text_done, 4)
    next(fore_t)
    flush(returned)
    next(fore_t)
    next(fore_t)
    next(fore_t)
    last_i = []
    for side, (span, _, ri, zi_s, zi_r) in enumerate(sides):
        if side == 1:
            next(fore_t)
            before = len(started)
            total = s.t_sum[...]
            for j in range(8):
                s.xt[j] = padded(total[18 * j : 18 * j + 18], 24)
            last_t = over_xy(s.xt, s.xt_r)
        for copy in fore_i[side]:
            copy.wait_recv()
        whole = sum(ri[j].astype(F32) for j in range(7))
        for k in range(8):
            s.zi[k, :, span] = (
                s.head_i[pl.ds(pl.multiple_of(k * 192 + slot * 24, 8), 24), span] + whole[k * 24 : k * 24 + 24]
            )
            zi_s[k] = padded(s.zi[k, :, span], 32).astype(BF16)
        last_i.append([message(zi_s.at[zo(o)], zi_r.at[o - 1], to_z(o)) for o in (4, 3, 5, 2, 6, 1, 7)])
    flush(before)
    for copy in last_t:
        copy.wait_recv()
    out_t[...] = (s.xt[slot] + sum(s.xt_r[j] for j in range(7)))[0:18]
    for (span, _, _, _, zi_r), copies in zip(sides, last_i):
        for copy in copies:
            copy.wait_recv()
        out_i[:, span] = s.zi[z, :, span] + sum(zi_r[j].astype(F32) for j in range(7))[0:24]
    flush(len(started))


def body(image_feats, text_feats, image_head, text_head, log_temp, logit_bias):
    vmem = pl.BlockSpec(memory_space=pltpu.VMEM)
    smem = pl.BlockSpec(memory_space=pltpu.SMEM)
    anywhere = pl.BlockSpec(memory_space=pl.ANY)
    scratch = scratch_of()

    def run(*refs):
        kernel(tuple(scratch), *refs)

    found = pl.pallas_call(
        run,
        out_shape=(jax.ShapeDtypeStruct((24, W), F32), jax.ShapeDtypeStruct((18, W), F32)),
        in_specs=[anywhere, anywhere, anywhere, anywhere, smem, smem],
        out_specs=(vmem, vmem),
        scratch_shapes=list(scratch.values()),
        compiler_params=pltpu.CompilerParams(
            collective_id=0, has_side_effects=True, vmem_limit_bytes=56 * 1024 * 1024
        ),
        name="pair_loss",
    )(image_feats, text_feats, image_head, text_head, log_temp, logit_bias)

    def hand_over(a, b, c, d):
        c[...] = a[...]
        d[...] = b[...]

    return pl.pallas_call(
        hand_over,
        out_shape=(jax.ShapeDtypeStruct((24, W), F32), jax.ShapeDtypeStruct((18, W), F32)),
        in_specs=[vmem, vmem],
        out_specs=(vmem, vmem),
        name="hand_over",
    )(*found)


def solution(mesh):
    placed = (P("dp", None), P("dp", None), P(None, "mp"), P(None, "mp"), P(), P())
    return jax.shard_map(
        body, mesh=mesh, in_specs=placed, out_specs=(P("dp", "mp"), P("dp", "mp")), check_vma=False
    )
```
